32 devices in a mesh: wide: 8 (over z, y), narrow: 4 (over x, core).
Axes of the slice: x: 2, y: 2, z: 4, core: 2. Of those that a mesh axis runs over, the one named last changes fastest.
Arguments:
- a_blocks: bfloat16 [6144, 64, 512], P(('wide', 'narrow')), may hold values from -0.25 to 0.25
- a_columns: int32 [6144, 8], P(('wide', 'narrow')), may hold values from 0 to 6143, as said below
- p_blocks: bfloat16 [6144, 64, 192], P(('wide', 'narrow')), may hold values from -0.75 to 0.75
- p_pattern: int32 [6144, 3], P(('wide', 'narrow')), may hold values from 0 to 1, as said below
- aggregate: int32 [6144], P(('wide', 'narrow')), may hold values from 0 to 63, as said below
- owner_map: int32 [64], replicated, may hold values from 0 to 31, as said below
Outputs:
- owned_coarse: bfloat16 [256, 64, 192], P(('wide', 'narrow'))
The draws below stay inside these ranges and needn't reach their ends.
Inputs may be any that keep to these rules, and one draw needn't show every extreme that they name: `a_columns`: entry 0 of row i is i; every entry lies within 32 rows of i; entries 1 and 2 are i - 32 and i + 32, clipped to 0 to 6143. `aggregate`: Non-decreasing; the aligned block of rows g * 192 to (g + 1) * 192 - 1 holds exactly aggregates g * 2 to (g + 1) * 2 - 1, each a run of 48 rows or more. `p_pattern`: entry 1 is always 1; entry 0 can be 1 only on the first 8 rows of an aggregate other than aggregate 0, entry 2 only on the last 8 rows of an aggregate other than the last one. `owner_map`: with N devices, N / 8 devices own exactly 8 aggregates each, N - N / 2 devices own exactly 2 each, and the others none; which devices is drawn.
All inputs are finite; a program needn't handle non-finite values.
Results may differ from the reference program's by a relative error of at most 0.005.
Values may be sent and summed in bfloat16 or wider, within the bound.
A program may use at most 128 MiB of HBM per device.

```python
import math
import jax
import jax.numpy as jnp
from jax import lax

B = 64
KA = 8
HR = 32
SPR = 8
LW = 2
OWNMAX = 8
R = 192
AMIN = 48
NB = 6144
NAGG = 64
N_WIDE = 8
N_NARROW = 4


def aggregate_layout(key):
    device_total = NAGG // LW
    spare_rows = R - LW * AMIN
    weights = jax.random.randint(jax.random.fold_in(key, 11), (device_total, LW), 1, 9)
    weights = weights.at[0, 0].set(0)
    cumulative = jnp.cumsum(weights, axis=1)
    before = cumulative - weights
    weight_total = cumulative[:, -1:]
    starts = AMIN * jnp.arange(LW, dtype=jnp.int32)[None, :] + spare_rows * before // weight_total
    row_ids = jnp.arange(R, dtype=jnp.int32)
    local_agg = jnp.sum((row_ids[None, :, None] >= starts[:, None, :]).astype(jnp.int32), axis=2) - 1
    ends = jnp.concatenate([starts[:, 1:], jnp.full((device_total, 1), R, jnp.int32)], axis=1)
    start_of = jnp.take_along_axis(starts, local_agg, axis=1)
    end_of = jnp.take_along_axis(ends, local_agg, axis=1)
    global_agg = local_agg + LW * jnp.arange(device_total, dtype=jnp.int32)[:, None]
    coin_flips = jax.random.randint(jax.random.fold_in(key, 12), (device_total, R, 3), 0, 2)
    near_start = row_ids[None, :] - start_of < SPR
    near_end = end_of - 1 - row_ids[None, :] < SPR
    lower_link = coin_flips[:, :, 0] * (near_start & (global_agg > 0)).astype(jnp.int32)
    upper_link = coin_flips[:, :, 2] * (near_end & (global_agg < NAGG - 1)).astype(jnp.int32)
    middle_link = jnp.ones_like(lower_link)
    pattern = jnp.stack([lower_link, middle_link, upper_link], axis=-1).astype(jnp.int32)
    return (global_agg.reshape(-1).astype(jnp.int32), pattern.reshape(-1, 3))


def draw_aggregate(key, part):
    return aggregate_layout(key)[0]


def draw_p_pattern(key, part):
    return aggregate_layout(key)[1]


def draw_a_columns(key, part):
    offsets = jax.random.randint(jax.random.fold_in(key, 21), (NB, KA), -HR, HR + 1)
    offsets = offsets.at[:, 0].set(0).at[:, 1].set(-HR).at[:, 2].set(HR)
    columns = jnp.arange(NB, dtype=jnp.int32)[:, None] + offsets
    return jnp.clip(columns, 0, NB - 1).astype(jnp.int32)


def draw_owner_map(key, part):
    device_total = NAGG // LW
    order = jax.random.permutation(jax.random.fold_in(key, 31), device_total).astype(jnp.int32)
    busy_total = device_total // OWNMAX
    ticket = jnp.arange(NAGG, dtype=jnp.int32)
    heavy_pick = jnp.clip(ticket // OWNMAX, 0, device_total - 1)
    light_pick = jnp.clip(busy_total + (ticket - device_total) // LW, 0, device_total - 1)
    holder = jnp.where(ticket < device_total, order[heavy_pick], order[light_pick])
    shuffle = jax.random.permutation(jax.random.fold_in(key, 32), NAGG)
    return holder[shuffle].astype(jnp.int32)


def block_scale(key, dims, split, low, high):
    factor_of = 1.0
    for position, shards_of in split:
        steps = jax.random.uniform(jax.random.fold_in(jax.random.fold_in(key, 6), position), (shards_of,), jnp.float32, low / len(split), high / len(split))
        factor_of = factor_of * jnp.repeat(jnp.exp(steps), dims[position] // shards_of).reshape((-1,) + (1,) * (len(dims) - 1 - position))
    return factor_of


def scatter_about(own_key, shape, width, most, split=(), kind=jnp.bfloat16):
    level = block_scale(own_key, shape, split, -0.22, 0.18) if split else 1.0
    drawn = jax.random.normal(own_key, shape, jnp.float32) * width * level
    return jnp.minimum(jnp.maximum(drawn, -most), most).astype(kind)


def setup_inputs(seed: int = 0) -> dict:
    splits = jax.random.split(jax.random.key(seed), 7)
    return {
        "a_blocks": scatter_about(splits[0], (NB, B, KA * B), (KA * B) ** -0.5, 0.25, ((0, 32),)),
        "a_columns": draw_a_columns(jax.random.fold_in(splits[6], 71), 0),
        "p_blocks": scatter_about(splits[2], (NB, B, 3 * B), B ** -0.5, 0.75, ((0, 32),)),
        "p_pattern": draw_p_pattern(jax.random.fold_in(splits[6], 71), 0),
        "aggregate": draw_aggregate(jax.random.fold_in(splits[6], 71), 0),
        "owner_map": draw_owner_map(jax.random.fold_in(splits[6], 71), 0),
    }


def reference(a_blocks, a_columns, p_blocks, p_pattern, aggregate, owner_map):
    device_total = N_WIDE * N_NARROW
    fine_total = a_blocks.shape[0]
    row_block = math.gcd(fine_total, 64)
    block_count = fine_total // row_block
    term_ids = jnp.arange(3, dtype=jnp.int32)

    def fetch_prolong(row_list):
        blocks = jnp.take(p_blocks, row_list, axis=0).astype(jnp.float32)
        blocks = blocks.reshape(row_list.shape + (B, 3, B))
        present = jnp.take(p_pattern, row_list, axis=0).astype(jnp.float32)
        return blocks * present[..., None, :, None]

    def accumulate_block(accum, block_index):
        first_row = (block_index * row_block).astype(jnp.int32)
        row_ids = first_row + jnp.arange(row_block, dtype=jnp.int32)
        a_part = lax.dynamic_slice_in_dim(a_blocks, first_row, row_block, 0).astype(jnp.float32)
        a_part = a_part.reshape(row_block, B, KA, B)
        col_part = jnp.take(a_columns, row_ids, axis=0)
        own_agg = jnp.take(aggregate, row_ids)
        far_agg = jnp.take(aggregate, col_part)
        own_p = fetch_prolong(row_ids)
        far_p = fetch_prolong(col_part)
        terms = jnp.einsum("inkx,ikxty->inkty", a_part, far_p)
        band = far_agg[:, :, None] + term_ids[None, None, :] - own_agg[:, None, None]
        chooser = (band[:, :, :, None] == term_ids[None, None, None, :]).astype(jnp.float32)
        applied = jnp.einsum("inkty,ikte->iney", terms, chooser).astype(jnp.bfloat16)
        applied = lax.optimization_barrier(applied).astype(jnp.float32)
        coarse = jnp.einsum("ixty,ixez->iteyz", own_p, applied)
        coarse_row = own_agg[:, None] + term_ids[None, :] - 1
        offset = term_ids[None, :] - term_ids[:, None] + 1
        inside = (offset[None] >= 0) & (offset[None] <= 2) & (coarse_row[:, :, None] >= 0) & (coarse_row[:, :, None] < NAGG)
        segment = jnp.where(inside, coarse_row[:, :, None] * 3 + offset[None], NAGG * 3)
        accum = accum + jax.ops.segment_sum(coarse.reshape(row_block * 9, B, B), segment.reshape(row_block * 9), num_segments=NAGG * 3 + 1)
        return accum, None

    start_accum = jnp.zeros((NAGG * 3 + 1, B, B), jnp.float32)
    accum, _ = lax.scan(accumulate_block, start_accum, jnp.arange(block_count, dtype=jnp.int32))
    coarse_rows = accum[:NAGG * 3].reshape(NAGG, 3, B, B).transpose(0, 2, 1, 3).reshape(NAGG, B, 3 * B)
    coarse_rows = coarse_rows.astype(jnp.bfloat16)
    one_hot = (owner_map[:, None] == jnp.arange(device_total, dtype=jnp.int32)[None, :]).astype(jnp.int32)
    owned_rank = jnp.sum(jnp.cumsum(one_hot, axis=0) * one_hot, axis=1) - 1
    placing = owner_map * OWNMAX + owned_rank
    result = jnp.zeros((device_total * OWNMAX, B, 3 * B), jnp.bfloat16).at[placing].set(coarse_rows)
    return result
```

```python
import jax
import jax.numpy as jnp
from jax import lax
from jax.experimental import pallas as pl
from jax.experimental.pallas import tpu as pltpu
from jax.sharding import PartitionSpec as P

HR = 32
LW = 2
OWNMAX = 8
GROUP = 16
SPR = 8
TEAM = 8
AXES = ("wide", "narrow")
MESH = pl.DeviceIdType.MESH
BF16 = jnp.bfloat16
F32 = jnp.float32


def kernel(a_hbm, cols, p_hbm, pattern, aggregate, owners, out,
           a_v, p_v, pooled, applied, sums, packed, rim, rim_side, edge_out, edge_in,
           piece_out, piece_in, spread, mail_out, mail_in, table_v, table,
           a_sem, p_sem, rim_send, rim_recv, edge_send, edge_recv,
           piece_send, piece_recv, spread_send, spread_recv, mail_send, mail_recv, table_sem):
    rows, nodes = a_hbm.shape[0], a_hbm.shape[1]
    me = lax.axis_index(AXES)
    narrow = lax.axis_size("narrow")
    count = lax.axis_size(AXES)
    teams = count // TEAM
    team, seat = me // TEAM, lax.rem(me, TEAM)
    groups = rows // GROUP

    def place_of(device):
        return (device // narrow, lax.rem(device, narrow))

    def mate(d):
        return team * TEAM + lax.rem(seat + d, TEAM)

    def peer(d):
        return lax.rem(team + d, teams) * TEAM + seat

    around = [place_of(lax.rem(me + 1, count)), place_of(lax.rem(me + count - 1, count))]
    barrier = pltpu.get_barrier_semaphore()
    for other in around:
        pl.semaphore_signal(barrier, inc=1, device_id=other, device_id_type=MESH)

    @pl.loop(1, TEAM)
    def _(d):
        pl.semaphore_signal(barrier, inc=1, device_id=place_of(mate(d)), device_id_type=MESH)

    @pl.loop(1, teams)
    def _(d):
        pl.semaphore_signal(barrier, inc=1, device_id=place_of(peer(d)), device_id_type=MESH)

    def p_copy(g):
        span = pl.ds(g * GROUP, GROUP)
        return pltpu.make_async_copy(p_hbm.at[span], p_v.at[span], p_sem.at[g])

    def a_copy(g):
        span = pl.ds(g * GROUP, GROUP)
        return pltpu.make_async_copy(a_hbm.at[span], a_v.at[span], a_sem.at[g])

    ends = (0, 1, groups - 2, groups - 1)
    middle = tuple(range(2, groups - 2))
    inner = tuple(range(3, groups - 3))
    for g in ends + middle:
        p_copy(g).start()
    for g in inner + (0, groups - 1, 1, 2, groups - 3, groups - 2):
        a_copy(g).start()

    total_agg = owners.shape[1]
    down = lax.broadcasted_iota(jnp.int32, (total_agg, total_agg), 0)
    over = lax.broadcasted_iota(jnp.int32, (total_agg, total_agg), 1)
    owner_row = owners[...]
    owner_col = jnp.sum(jnp.where(down == over, owner_row, 0), axis=1, keepdims=True)
    rank = jnp.sum(jnp.where((owner_col == owner_row) & (over < down), 1, 0), axis=1, keepdims=True)
    wanted = lax.broadcasted_iota(jnp.int32, (total_agg, 128), 1) + team * (TEAM * OWNMAX)
    number = lax.broadcasted_iota(jnp.int32, (total_agg, 128), 0) + 1
    hit = (owner_col * OWNMAX + rank) == wanted
    found = jnp.sum(jnp.where(hit, number, 0), axis=0, keepdims=True)
    table_v[...] = jnp.broadcast_to(found, table_v.shape)
    table_copy = pltpu.make_async_copy(table_v, table, table_sem)
    table_copy.start()

    left = lax.broadcasted_iota(jnp.int32, (nodes, 128), 1) < 64
    lane = lax.broadcasted_iota(jnp.int32, (1, 128), 1) < 64

    def place_group(g, at_end):
        for j in range(GROUP):
            i = g * GROUP + j
            second = jnp.where(aggregate[i] - me * LW == 1, 1.0, 0.0)
            has0 = pattern[0, i].astype(F32)
            has2 = pattern[2, i].astype(F32)
            x0 = p_v[i, :, :128]
            x2 = p_v[i, :, 128:]
            swapped = jnp.concatenate([x0[:, 64:], x0[:, :64]], axis=1)
            mixed = jnp.concatenate([x2, x0[:, 64:]], axis=1)
            one = jnp.where(lane, second, second * has0).astype(BF16)
            two = jnp.where(lane, (1.0 - second) * has2, 1.0 - second).astype(BF16)
            pooled[HR + i, :, :128] = swapped * one + mixed * two
            if at_end:
                three = jnp.where(lane, (1.0 - second) * has0, second * has2).astype(BF16)
                pooled[HR + i, :, 128:] = jnp.concatenate([x0[:, :64], x2], axis=1) * three
            else:
                pooled[HR + i, :, 128:] = jnp.zeros_like(x0)

    def rim_copies(side):
        end = pl.ds(rows + HR - SPR if side == 0 else HR, SPR)
        pairs = (
            (packed.at[side], rim.at[side]),
            (pooled.at[end, :, pl.ds(128, 128)], rim_side.at[side]),
        )
        return [
            pltpu.make_async_remote_copy(
                src_ref=source,
                dst_ref=landing,
                send_sem=rim_send.at[side, half],
                recv_sem=rim_recv.at[side, half],
                device_id=around[side],
                device_id_type=MESH,
            )
            for half, (source, landing) in enumerate(pairs)
        ]

    for g in ends:
        p_copy(g).wait()

    @pl.loop(0, 2)
    def _(end):
        place_group(end * (groups - 1), True)

    @pl.loop(0, HR // 2)
    def _(i):
        for side, first in ((0, rows - HR), (1, 0)):
            packed[side, i] = jnp.concatenate(
                [p_v[first + i + k, :, 64:128] for k in (0, HR // 2)], axis=1
            )

    pl.semaphore_wait(barrier, 2 + TEAM - 1 + teams - 1)
    copies = rim_copies(0) + rim_copies(1)
    for copy in copies:
        copy.start()

    @pl.loop(0, 2)
    def _(end):
        place_group(1 + end * (groups - 3), False)

    @pl.loop(2, groups - 2)
    def _(g):
        p_copy(g).wait()
        place_group(g, False)

    sums[...] = jnp.zeros_like(sums)
    base = HR - me * rows

    def apply_rows(first, buffer, width):
        for j in range(GROUP):
            i = first + j
            stack = jnp.concatenate(
                [pooled[jnp.maximum(cols[k, i] + base, 0), :, :width] for k in range(8)], axis=0
            )
            product = jnp.dot(a_v[i], stack, preferred_element_type=F32)
            applied[buffer, j * nodes : (j + 1) * nodes, :width] = product.astype(BF16)

    def add_up(first, buffer, high, width):
        left_rows = pooled[pl.ds(HR + first, GROUP), :, :high].reshape(GROUP * nodes, high)
        sums[:high, :width] += lax.dot_general(
            left_rows, applied[buffer, :, :width], (((0,), (0,)), ((), ())),
            preferred_element_type=F32,
        )

    def run_pair(first, later, high, width):
        apply_rows(first, 0, width)
        apply_rows(later, 1, width)
        add_up(first, 0, high, width)
        add_up(later, 1, high, width)

    @pl.loop(0, len(inner) // 2)
    def _(step):
        g = inner[0] + 2 * step
        a_copy(g).wait()
        a_copy(g + 1).wait()
        run_pair(g * GROUP, (g + 1) * GROUP, 128, 128)

    for copy in copies:
        copy.wait()

    @pl.loop(0, HR // 2)
    def _(i):
        zero = jnp.zeros((nodes, 128), BF16)
        for side, first in enumerate((0, rows + HR)):
            both = rim[side, i]
            swapped = jnp.concatenate([both[:, 64:], both[:, :64]], axis=1)
            keep = left if side == 0 else ~left
            early, late = (both, swapped) if side == 0 else (swapped, both)
            for k, own in ((0, early), (HR // 2, late)):
                pooled[first + i + k, :, :128] = zero
                pooled[first + i + k, :, 128:] = jnp.where(keep, own, zero)

    @pl.loop(0, SPR)
    def _(i):
        for side, first in enumerate((HR - SPR, rows + HR)):
            pooled[first + i, :, :128] = rim_side[side, i]

    a_copy(0).wait()
    a_copy(groups - 1).wait()
    run_pair(0, (groups - 1) * GROUP, 256, 256)

    edge_out[0, :, :64] = sums[192:, :64]
    edge_out[0, :, 64:] = sums[192:, 192:]
    edge_out[1, :, :64] = sums[128:192, 128:192]
    edge_out[1, :, 64:] = sums[128:192, 64:128]
    edges = [
        pltpu.make_async_remote_copy(
            src_ref=edge_out.at[side],
            dst_ref=edge_in.at[side],
            send_sem=edge_send.at[side],
            recv_sem=edge_recv.at[side],
            device_id=around[side],
            device_id_type=MESH,
        )
        for side in range(2)
    ]
    for edge in edges:
        edge.start()

    @pl.loop(0, 2)
    def _(side):
        g = 1 + side * (groups - 4)
        a_copy(g).wait()
        a_copy(g + 1).wait()
        run_pair(g * GROUP, (g + 1) * GROUP, 128, 256)

    for edge in edges:
        edge.wait()
    table_copy.wait()

    before, after = edge_in[0], edge_in[1]
    front0 = jnp.concatenate([sums[64:128, 128:192], sums[64:128, 64:128]], axis=1) + before
    front1 = jnp.concatenate([sums[:64, 64:128], sums[:64, :64] + after[:, :64]], axis=1)
    tails = jnp.concatenate([sums[64:128, :64], sums[:64, 192:] + after[:, 64:]], axis=1)
    lines = nodes // TEAM
    for t, part in enumerate((front0, front1, tails)):
        piece_out[:, t * lines : (t + 1) * lines, :] = part.reshape(TEAM, lines, 128)
    piece_in[seat] = piece_out[seat]

    def piece_copy(d):
        there = lax.rem(seat + d, TEAM)
        return pltpu.make_async_remote_copy(
            src_ref=piece_out.at[there],
            dst_ref=piece_in.at[seat],
            send_sem=piece_send.at[d],
            recv_sem=piece_recv.at[d],
            device_id=place_of(mate(d)),
            device_id_type=MESH,
        )

    @pl.loop(1, TEAM)
    def _(d):
        piece_copy(d).start()

    @pl.loop(1, TEAM)
    def _(d):
        piece_copy(d).wait()

    for pair in range(TEAM // 2):
        one, two = piece_in[2 * pair], piece_in[2 * pair + 1]
        spread[team, 3 * pair] = one[: 2 * lines].astype(BF16)
        spread[team, 3 * pair + 1] = two[: 2 * lines].astype(BF16)
        spread[team, 3 * pair + 2] = jnp.concatenate(
            [one[2 * lines :], two[2 * lines :]], axis=0
        ).astype(BF16)

    def spread_copy(d):
        return pltpu.make_async_remote_copy(
            src_ref=spread.at[team],
            dst_ref=spread.at[team],
            send_sem=spread_send.at[d],
            recv_sem=spread_recv.at[d],
            device_id=place_of(peer(d)),
            device_id_type=MESH,
        )

    @pl.loop(1, teams)
    def _(d):
        spread_copy(d).start()

    @pl.loop(1, teams)
    def _(d):
        spread_copy(d).wait()

    def fill(there, box):
        fronts, ends_of = [], []
        for s in range(OWNMAX):
            entry = table[0, there * OWNMAX + s]
            agg = jnp.maximum(entry - 1, 0)
            source = agg // LW
            which = lax.rem(agg, LW)
            from_team = source // TEAM
            member = lax.rem(source, TEAM)
            pair, half = member // 2, lax.rem(member, 2)
            front = spread[from_team, 3 * pair + half].astype(F32)
            front = jnp.where(which == 1, front[lines:], front[:lines])
            fronts.append(jnp.where(entry > 0, front, 0.0))
            tail = spread[from_team, 3 * pair + 2].astype(F32)
            tail = jnp.where(half == 1, tail[lines:], tail[:lines])
            swapped = jnp.concatenate([tail[:, 64:], tail[:, :64]], axis=1)
            tail = jnp.where(which == s % 2, tail, swapped)
            ends_of.append(jnp.where(entry > 0, tail, 0.0))
        for k in range(OWNMAX // 2):
            box[k] = jnp.concatenate(fronts[2 * k : 2 * k + 2], axis=0).astype(BF16)
        low = lax.broadcasted_iota(jnp.int32, (lines, 128), 1) < 64
        tails = [jnp.where(low, ends_of[2 * k], ends_of[2 * k + 1]) for k in range(OWNMAX // 2)]
        for k in range(OWNMAX // 4):
            box[OWNMAX // 2 + k] = jnp.concatenate(tails[2 * k : 2 * k + 2], axis=0).astype(BF16)

    def mail_copy(d):
        return pltpu.make_async_remote_copy(
            src_ref=mail_out.at[d],
            dst_ref=mail_in.at[seat],
            send_sem=mail_send.at[d],
            recv_sem=mail_recv.at[d],
            device_id=place_of(mate(d)),
            device_id_type=MESH,
        )

    @pl.loop(1, TEAM)
    def _(d):
        fill(lax.rem(seat + d, TEAM), mail_out.at[d])
        mail_copy(d).start()

    fill(seat, mail_in.at[seat])

    @pl.loop(1, TEAM)
    def _(d):
        mail_copy(d).wait()

    for m in range(TEAM // 2):
        span = pl.ds(2 * lines * m, 2 * lines)
        for k in range(OWNMAX // 2):
            one, two = (mail_in[2 * m + q, k].astype(F32) for q in range(2))
            for h in range(2):
                part = slice(h * lines, (h + 1) * lines)
                out[2 * k + h, span, :128] = jnp.concatenate([one[part], two[part]], axis=0).astype(BF16)
        for k in range(OWNMAX // 4):
            one, two = (mail_in[2 * m + q, OWNMAX // 2 + k].astype(F32) for q in range(2))
            for h in range(2):
                part = slice(h * lines, (h + 1) * lines)
                both = jnp.concatenate([one[part], two[part]], axis=0).astype(BF16)
                out[4 * k + 2 * h, span, 128:] = both[:, :64]
                out[4 * k + 2 * h + 1, span, 128:] = both[:, 64:]


def shards(a_blocks, a_columns, p_blocks, p_pattern, aggregate, owner_map):
    rows, nodes = a_blocks.shape[:2]
    teams = lax.axis_size(AXES) // TEAM
    vmem = pl.BlockSpec(memory_space=pltpu.VMEM)
    smem = pl.BlockSpec(memory_space=pltpu.SMEM)
    hbm = pl.BlockSpec(memory_space=pl.ANY)
    groups = rows // GROUP
    lines = nodes // TEAM
    half = OWNMAX // 2 + OWNMAX // 4
    dma = pltpu.SemaphoreType.DMA
    return pl.pallas_call(
        kernel,
        out_shape=jax.ShapeDtypeStruct((OWNMAX, nodes, 3 * nodes), BF16),
        in_specs=[hbm, smem, hbm, smem, smem, vmem],
        out_specs=vmem,
        scratch_shapes=[
            pltpu.VMEM(a_blocks.shape, BF16),
            pltpu.VMEM(p_blocks.shape, BF16),
            pltpu.VMEM((rows + 2 * HR, nodes, 4 * nodes), BF16),
            pltpu.VMEM((2, GROUP * nodes, 4 * nodes), BF16),
            pltpu.VMEM((4 * nodes, 4 * nodes), F32),
            pltpu.VMEM((2, HR // 2, nodes, 2 * nodes), BF16),
            pltpu.VMEM((2, HR // 2, nodes, 2 * nodes), BF16),
            pltpu.VMEM((2, SPR, nodes, 2 * nodes), BF16),
            pltpu.VMEM((2, nodes, 2 * nodes), F32),
            pltpu.VMEM((2, nodes, 2 * nodes), F32),
            pltpu.VMEM((TEAM, 3 * lines, 128), F32),
            pltpu.VMEM((TEAM, 3 * lines, 128), F32),
            pltpu.VMEM((teams, 3 * TEAM // 2, 2 * lines, 128), BF16),
            pltpu.VMEM((TEAM, half, 2 * lines, 128), BF16),
            pltpu.VMEM((TEAM, half, 2 * lines, 128), BF16),
            pltpu.VMEM((8, 128), jnp.int32),
            pltpu.SMEM((8, 128), jnp.int32),
            dma((groups,)),
            dma((groups,)),
            dma((2, 2)),
            dma((2, 2)),
            dma((2,)),
            dma((2,)),
            dma((TEAM,)),
            dma((TEAM,)),
            dma((teams,)),
            dma((teams,)),
            dma((TEAM,)),
            dma((TEAM,)),
            dma,
        ],
        compiler_params=pltpu.CompilerParams(
            collective_id=0, has_side_effects=True, vmem_limit_bytes=56 << 20
        ),
    )(a_blocks, a_columns.T, p_blocks, p_pattern.T, aggregate, owner_map[None])


def solution(mesh):
    placed = (
        P(AXES, None, None),
        P(AXES, None),
        P(AXES, None, None),
        P(AXES, None),
        P(AXES),
        P(),
    )
    return jax.shard_map(
        shards,
        mesh=mesh,
        in_specs=placed,
        out_specs=P(AXES, None, None),
        check_vma=False,
    )
```

```python
import jax
import jax.numpy as jnp
from jax import lax
from jax.experimental import pallas as pl
from jax.experimental.pallas import tpu as pltpu
from jax.sharding import PartitionSpec as P

HR = 32
LW = 2
OWNMAX = 8
GROUP = 16
SPR = 8
TEAM = 8
AXES = ("wide", "narrow")
MESH = pl.DeviceIdType.MESH
BF16 = jnp.bfloat16
F32 = jnp.float32


def kernel(a_hbm, cols_hbm, p_hbm, pattern_hbm, aggregate_hbm, owners_hbm, out,
           cols, pattern, aggregate, owners, a_v, p_v, pooled, applied, sums, packed, packed_side,
           rim, rim_side, edge_out, edge_in, piece_out, spread, mail_out, mail_in, table_v, table,
           a_sem, p_sem, index_sem, rim_send, rim_recv, edge_send, edge_recv,
           piece_send, piece_recv, mail_send, mail_recv, vouch):
    rows, nodes = a_hbm.shape[0], a_hbm.shape[1]
    me = lax.axis_index(AXES)
    narrow = lax.axis_size("narrow")
    count = lax.axis_size(AXES)
    teams = count // TEAM
    rounds = teams.bit_length() - 1
    team, seat = me // TEAM, lax.rem(me, TEAM)
    groups = rows // GROUP
    has_before, has_after = me > 0, me < count - 1

    def place_of(device):
        return (device // narrow, lax.rem(device, narrow))

    def mate(d):
        return team * TEAM + lax.rem(seat + d, TEAM)

    def partner(r):
        step = 1 << r
        up = lax.rem(team // step, 2) == 0
        return place_of(jnp.where(up, team + step, team - step) * TEAM + seat)

    after = place_of(jnp.minimum(me + 1, count - 1))
    before = place_of(jnp.maximum(me - 1, 0))
    barrier = pltpu.get_barrier_semaphore()

    @pl.when(has_after)
    def _():
        pl.semaphore_signal(barrier, inc=1, device_id=after, device_id_type=MESH)

    @pl.when(has_before)
    def _():
        pl.semaphore_signal(barrier, inc=1, device_id=before, device_id_type=MESH)

    for r in range(rounds):
        pl.semaphore_signal(barrier, inc=1, device_id=partner(r), device_id_type=MESH)

    @pl.loop(1, TEAM)
    def _(d):
        pl.semaphore_signal(barrier, inc=1, device_id=place_of(mate(d)), device_id_type=MESH)

    def p_copy(g):
        span = pl.ds(g * GROUP, GROUP)
        return pltpu.make_async_copy(p_hbm.at[span], p_v.at[span], p_sem.at[g])

    def a_copy(g):
        span = pl.ds(g * GROUP, GROUP)
        return pltpu.make_async_copy(a_hbm.at[span], a_v.at[span], a_sem.at[g])

    index_copies = [
        pltpu.make_async_copy(source, landing, index_sem.at[k])
        for k, (source, landing) in enumerate(
            (
                (pattern_hbm, pattern),
                (aggregate_hbm, aggregate),
                (owners_hbm, owners),
                (cols_hbm, cols),
            )
        )
    ]
    for copy in index_copies:
        copy.start()
    ends = (0, 1, groups - 2, groups - 1)
    middle = tuple(range(2, groups - 2))
    inner = tuple(range(3, groups - 3))
    for g in ends + middle:
        p_copy(g).start()
    for g in inner + (2, groups - 3, 0, groups - 1, 1, groups - 2):
        a_copy(g).start()

    left = lax.broadcasted_iota(jnp.int32, (nodes, 128), 1) < 64
    lane = lax.broadcasted_iota(jnp.int32, (1, 128), 1) < 64

    def place_group(g, at_end):
        for j in range(GROUP):
            i = g * GROUP + j
            second = jnp.where(aggregate[0, i] - me * LW == 1, 1.0, 0.0)
            has0 = pattern[0, i].astype(F32)
            has2 = pattern[2, i].astype(F32)
            x0 = p_v[i, :, :128]
            x2 = p_v[i, :, 128:]
            swapped = jnp.concatenate([x0[:, 64:], x0[:, :64]], axis=1)
            mixed = jnp.concatenate([x2, x0[:, 64:]], axis=1)
            one = jnp.where(lane, second, second * has0).astype(BF16)
            two = jnp.where(lane, (1.0 - second) * has2, 1.0 - second).astype(BF16)
            pooled[HR + i, :, :128] = swapped * one + mixed * two
            if at_end:
                three = jnp.where(lane, (1.0 - second) * has0, second * has2).astype(BF16)
                pooled[HR + i, :, 128:] = jnp.concatenate([x0[:, :64], x2], axis=1) * three
            else:
                pooled[HR + i, :, 128:] = jnp.zeros_like(x0)

    for copy in index_copies:
        copy.wait()

    total_agg = owners.shape[1]
    down = lax.broadcasted_iota(jnp.int32, (total_agg, total_agg), 0)
    over = lax.broadcasted_iota(jnp.int32, (total_agg, total_agg), 1)
    owner_row = owners[...]
    owner_col = jnp.sum(jnp.where(down == over, owner_row, 0), axis=1, keepdims=True)
    rank = jnp.sum(jnp.where((owner_col == owner_row) & (over < down), 1, 0), axis=1, keepdims=True)
    wanted = lax.broadcasted_iota(jnp.int32, (total_agg, 128), 1) + team * (TEAM * OWNMAX)
    number = lax.broadcasted_iota(jnp.int32, (total_agg, 128), 0) + 1
    hit = (owner_col * OWNMAX + rank) == wanted
    found = jnp.sum(jnp.where(hit, number, 0), axis=0, keepdims=True)
    table_v[...] = jnp.broadcast_to(found, table_v.shape)
    table_copy = pltpu.make_async_copy(table_v, table, index_sem.at[4])
    table_copy.start()

    for g in ends:
        p_copy(g).wait()

    @pl.loop(0, 2)
    def _(end):
        place_group(end * (groups - 1), True)

    @pl.loop(0, HR // 2)
    def _(i):
        for side, first in ((0, rows - HR), (1, 0)):
            packed[side, i] = jnp.concatenate(
                [p_v[first + i + k, :, 64:128] for k in (0, HR // 2)], axis=1
            )

    @pl.loop(0, SPR // 2)
    def _(i):
        for side, first, at in ((0, HR + rows - SPR, 192), (1, HR, 128)):
            packed_side[side, i] = jnp.concatenate(
                [pooled[first + i + k, :, at : at + 64] for k in (0, SPR // 2)], axis=1
            )

    near = TEAM - 1 + rounds + jnp.where(has_after, 1, 0) + jnp.where(has_before, 1, 0)
    pl.semaphore_wait(barrier, near)

    def rim_copies(side):
        pairs = ((packed.at[side], rim.at[side]), (packed_side.at[side], rim_side.at[side]))
        return [
            pltpu.make_async_remote_copy(
                src_ref=source,
                dst_ref=landing,
                send_sem=rim_send.at[side, half],
                recv_sem=rim_recv.at[side, half],
                device_id=(after, before)[side],
                device_id_type=MESH,
            )
            for half, (source, landing) in enumerate(pairs)
        ]

    sends = (has_after, has_before)
    receives = (has_before, has_after)
    rims = [rim_copies(side) for side in range(2)]
    for side in range(2):
        @pl.when(sends[side])
        def _():
            for copy in rims[side]:
                copy.start()

    def vouch_for(r):
        pl.semaphore_signal(vouch.at[r], inc=1, device_id=partner(r), device_id_type=MESH)

    vouch_for(0)

    @pl.loop(0, 2)
    def _(end):
        place_group(1 + end * (groups - 3), False)

    @pl.loop(2, groups - 2)
    def _(g):
        p_copy(g).wait()
        place_group(g, False)

    @pl.loop(0, HR)
    def _(i):
        pooled[i] = jnp.zeros((nodes, 256), BF16)
        pooled[rows + HR + i] = jnp.zeros((nodes, 256), BF16)

    sums[...] = jnp.zeros_like(sums)
    base = HR - me * rows

    def apply_rows(first, total, buffer, width):
        for j in range(total):
            i = first + j
            stack = jnp.concatenate(
                [pooled[jnp.maximum(cols[k, i] + base, 0), :, :width] for k in range(8)], axis=0
            )
            product = jnp.dot(a_v[i], stack, preferred_element_type=F32)
            applied[buffer, j * nodes : (j + 1) * nodes, :width] = product.astype(BF16)

    def add_up(first, total, buffer, high, width):
        left_rows = pooled[pl.ds(HR + first, total), :, :high].reshape(total * nodes, high)
        sums[:high, :width] += lax.dot_general(
            left_rows, applied[buffer, : total * nodes, :width], (((0,), (0,)), ((), ())),
            preferred_element_type=F32,
        )

    def run_pair(first, later, total, high, width):
        apply_rows(first, total, 0, width)
        apply_rows(later, total, 1, width)
        add_up(first, total, 0, high, width)
        add_up(later, total, 1, high, width)

    @pl.loop(0, len(inner) // 2)
    def _(step):
        g = inner[0] + 2 * step
        a_copy(g).wait()
        a_copy(g + 1).wait()
        run_pair(g * GROUP, (g + 1) * GROUP, GROUP, 128, 128)

    pl.semaphore_wait(vouch.at[0], 1)
    for r in range(1, rounds):
        vouch_for(r)
        if r < rounds - 1:
            pl.semaphore_wait(vouch.at[r], 1)

    a_copy(2).wait()
    a_copy(groups - 3).wait()
    run_pair(2 * GROUP, (groups - 3) * GROUP, GROUP, 128, 256)
    for g in ends:
        a_copy(g).wait()

    zero = jnp.zeros((nodes, 128), BF16)
    for side, first in enumerate((0, rows + HR)):
        @pl.when(receives[side])
        def _():
            for copy in rims[side]:
                copy.wait_recv()
            keep = left if side == 0 else ~left

            @pl.loop(0, HR // 2)
            def _(i):
                both = rim[side, i]
                swapped = jnp.concatenate([both[:, 64:], both[:, :64]], axis=1)
                early, late = (both, swapped) if side == 0 else (swapped, both)
                for k, own in ((0, early), (HR // 2, late)):
                    pooled[first + i + k, :, 128:] = jnp.where(keep, own, zero)

            start = HR - SPR if side == 0 else rows + HR

            @pl.loop(0, SPR // 2)
            def _(i):
                both = rim_side[side, i]
                swapped = jnp.concatenate([both[:, 64:], both[:, :64]], axis=1)
                early, late = (swapped, both) if side == 0 else (both, swapped)
                for k, own in ((0, early), (SPR // 2, late)):
                    pooled[start + i + k, :, :128] = jnp.where(keep, zero, own)

    run_pair(0, rows - SPR, SPR, 256, 256)

    edge_out[0, :, :64] = sums[192:, :64]
    edge_out[0, :, 64:] = sums[192:, 192:]
    edge_out[1, :, :64] = sums[128:192, 128:192]
    edge_out[1, :, 64:] = sums[128:192, 64:128]
    edges = [
        pltpu.make_async_remote_copy(
            src_ref=edge_out.at[side],
            dst_ref=edge_in.at[side],
            send_sem=edge_send.at[side],
            recv_sem=edge_recv.at[side],
            device_id=(after, before)[side],
            device_id_type=MESH,
        )
        for side in range(2)
    ]
    for side in range(2):
        @pl.when(sends[side])
        def _():
            edges[side].start()

    @pl.loop(0, 2)
    def _(side):
        first = SPR + side * (rows - HR - SPR)
        apply_rows(first, HR - SPR, 0, 256)
        add_up(first, HR - SPR, 0, 128, 256)

    table_copy.wait()
    if rounds:
        pl.semaphore_wait(vouch.at[rounds - 1], 1)
    for side in range(2):
        @pl.when(receives[side])
        def _():
            edges[side].wait_recv()

        @pl.when(~receives[side])
        def _():
            edge_in[side] = jnp.zeros((nodes, 128), F32)

    early, late = edge_in[0], edge_in[1]
    front0 = jnp.concatenate([sums[64:128, 128:192], sums[64:128, 64:128]], axis=1) + early
    front1 = jnp.concatenate([sums[:64, 64:128], sums[:64, :64] + late[:, :64]], axis=1)
    tails = jnp.concatenate([sums[64:128, :64], sums[:64, 192:] + late[:, 64:]], axis=1)
    lines = nodes // TEAM
    for s in range(TEAM):
        part = slice(s * lines, (s + 1) * lines)
        piece_out[s, : 2 * lines] = jnp.concatenate([front0[part], front1[part]], axis=0).astype(BF16)
        piece_out[s, 2 * lines :] = tails[part].astype(BF16)

    def piece_copy(d):
        there = lax.rem(me + d, count)
        return pltpu.make_async_remote_copy(
            src_ref=piece_out.at[lax.rem(there, TEAM)],
            dst_ref=spread.at[me],
            send_sem=piece_send.at[d],
            recv_sem=piece_recv.at[d],
            device_id=place_of(there),
            device_id_type=MESH,
        )

    @pl.loop(1, count)
    def _(d):
        piece_copy(d).start()

    spread[me] = piece_out[seat]

    @pl.loop(1, count)
    def _(d):
        piece_copy(d).wait_recv()

    low = lax.broadcasted_iota(jnp.int32, (lines, 128), 1) < 64

    def fill(there, box):
        fronts, ends_of = [], []
        for s in range(OWNMAX):
            entry = table[0, there * OWNMAX + s]
            agg = jnp.maximum(entry - 1, 0)
            which = lax.rem(agg, LW)
            piece = spread[agg // LW].astype(F32)
            front = jnp.where(which == 1, piece[lines : 2 * lines], piece[:lines])
            fronts.append(jnp.where(entry > 0, front, 0.0))
            tail = piece[2 * lines :]
            swapped = jnp.concatenate([tail[:, 64:], tail[:, :64]], axis=1)
            tail = jnp.where(which == s % 2, tail, swapped)
            ends_of.append(jnp.where(entry > 0, tail, 0.0))
        for k in range(OWNMAX // 2):
            box[k] = jnp.concatenate(fronts[2 * k : 2 * k + 2], axis=0).astype(BF16)
        tails = [jnp.where(low, ends_of[2 * k], ends_of[2 * k + 1]) for k in range(OWNMAX // 2)]
        for k in range(OWNMAX // 4):
            box[OWNMAX // 2 + k] = jnp.concatenate(tails[2 * k : 2 * k + 2], axis=0).astype(BF16)

    def mail_copy(d):
        return pltpu.make_async_remote_copy(
            src_ref=mail_out.at[d],
            dst_ref=mail_in.at[seat],
            send_sem=mail_send.at[d],
            recv_sem=mail_recv.at[d],
            device_id=place_of(mate(d)),
            device_id_type=MESH,
        )

    @pl.loop(1, TEAM)
    def _(d):
        fill(lax.rem(seat + d, TEAM), mail_out.at[d])
        mail_copy(d).start()

    fill(seat, mail_in.at[seat])

    @pl.loop(1, TEAM)
    def _(d):
        mail_copy(d).wait_recv()

    for m in range(TEAM // 2):
        span = pl.ds(2 * lines * m, 2 * lines)
        for k in range(OWNMAX // 2):
            one, two = (mail_in[2 * m + q, k].astype(F32) for q in range(2))
            for h in range(2):
                part = slice(h * lines, (h + 1) * lines)
                out[2 * k + h, span, :128] = jnp.concatenate([one[part], two[part]], axis=0).astype(BF16)
        for k in range(OWNMAX // 4):
            one, two = (mail_in[2 * m + q, OWNMAX // 2 + k].astype(F32) for q in range(2))
            for h in range(2):
                part = slice(h * lines, (h + 1) * lines)
                both = jnp.concatenate([one[part], two[part]], axis=0).astype(BF16)
                out[4 * k + 2 * h, span, 128:] = both[:, :64]
                out[4 * k + 2 * h + 1, span, 128:] = both[:, 64:]

    for side in range(2):
        @pl.when(sends[side])
        def _():
            for copy in rims[side] + [edges[side]]:
                copy.wait_send()

    @pl.loop(1, count)
    def _(d):
        piece_copy(d).wait_send()

    @pl.loop(1, TEAM)
    def _(d):
        mail_copy(d).wait_send()


def shards(a_blocks, a_columns, p_blocks, p_pattern, aggregate, owner_map):
    rows, nodes = a_blocks.shape[:2]
    count = lax.axis_size(AXES)
    vmem = pl.BlockSpec(memory_space=pltpu.VMEM)
    hbm = pl.BlockSpec(memory_space=pl.ANY)
    groups = rows // GROUP
    lines = nodes // TEAM
    half = OWNMAX // 2 + OWNMAX // 4
    dma = pltpu.SemaphoreType.DMA
    pool = (rows + 2 * HR, nodes, 4 * nodes)
    total_agg = owner_map.shape[0]
    return pl.pallas_call(
        kernel,
        out_shape=jax.ShapeDtypeStruct((OWNMAX, nodes, 3 * nodes), BF16),
        in_specs=[hbm] * 6,
        out_specs=vmem,
        scratch_shapes=[
            pltpu.SMEM((a_columns.shape[1], rows), jnp.int32),
            pltpu.SMEM((3, rows), jnp.int32),
            pltpu.SMEM((1, rows), jnp.int32),
            pltpu.VMEM((1, total_agg), jnp.int32),
            pltpu.VMEM(a_blocks.shape, BF16),
            pltpu.VMEM(p_blocks.shape, BF16),
            pltpu.VMEM(pool, BF16),
            pltpu.VMEM((2, (HR - SPR) * nodes, 4 * nodes), BF16),
            pltpu.VMEM((4 * nodes, 4 * nodes), F32),
            pltpu.VMEM((2, HR // 2, nodes, 2 * nodes), BF16),
            pltpu.VMEM((2, SPR // 2, nodes, 2 * nodes), BF16),
            pltpu.VMEM((2, HR // 2, nodes, 2 * nodes), BF16),
            pltpu.VMEM((2, SPR // 2, nodes, 2 * nodes), BF16),
            pltpu.VMEM((2, nodes, 2 * nodes), F32),
            pltpu.VMEM((2, nodes, 2 * nodes), F32),
            pltpu.VMEM((TEAM, 3 * lines, 128), BF16),
            pltpu.VMEM((count, 3 * lines, 128), BF16),
            pltpu.VMEM((TEAM, half, 2 * lines, 128), BF16),
            pltpu.VMEM((TEAM, half, 2 * lines, 128), BF16),
            pltpu.VMEM((8, 128), jnp.int32),
            pltpu.SMEM((8, 128), jnp.int32),
            dma((groups,)),
            dma((groups,)),
            dma((5,)),
            dma((2, 2)),
            dma((2, 2)),
            dma((2,)),
            dma((2,)),
            dma((count,)),
            dma((count,)),
            dma((TEAM,)),
            dma((TEAM,)),
            pltpu.SemaphoreType.REGULAR((max(count // TEAM - 1, 1).bit_length(),)),
        ],
        compiler_params=pltpu.CompilerParams(
            collective_id=0, has_side_effects=True, vmem_limit_bytes=56 << 20
        ),
    )(a_blocks, a_columns.T, p_blocks, p_pattern.T, aggregate[None], owner_map[None])


def solution(mesh):
    placed = (
        P(AXES, None, None),
        P(AXES, None),
        P(AXES, None, None),
        P(AXES, None),
        P(AXES),
        P(),
    )
    return jax.shard_map(
        shards,
        mesh=mesh,
        in_specs=placed,
        out_specs=P(AXES, None, None),
        check_vma=False,
    )
```

```python
import jax
import jax.numpy as jnp
from jax import lax
from jax.experimental import pallas as pl
from jax.experimental.pallas import tpu as pltpu
from jax.sharding import PartitionSpec as P

HR = 32
LW = 2
OWNMAX = 8
GROUP = 16
SPR = 8
TEAM = 8
AXES = ("wide", "narrow")
MESH = pl.DeviceIdType.MESH
BF16 = jnp.bfloat16
F32 = jnp.float32


def kernel(a_hbm, cols_hbm, p_hbm, pattern_hbm, aggregate_hbm, owners_hbm, out,
           cols, pattern, aggregate, owners, a_v, p_v, pooled, applied, sums, packed, packed_side,
           rim, rim_side, edge_out, edge_in, piece_out, spread, mail_out, mail_in, table_v, table,
           a_sem, p_sem, index_sem, rim_send, rim_recv, edge_send, edge_recv,
           piece_send, piece_recv, mail_send, mail_recv, vouch):
    rows, nodes = a_hbm.shape[0], a_hbm.shape[1]
    me = lax.axis_index(AXES)
    narrow = lax.axis_size("narrow")
    count = lax.axis_size(AXES)
    teams = count // TEAM
    rounds = teams.bit_length() - 1
    team, seat = me // TEAM, lax.rem(me, TEAM)
    groups = rows // GROUP
    has_before, has_after = me > 0, me < count - 1

    def place_of(device):
        return (device // narrow, lax.rem(device, narrow))

    def mate(d):
        return team * TEAM + lax.rem(seat + d, TEAM)

    def partner(r):
        step = 1 << r
        up = lax.rem(team // step, 2) == 0
        return place_of(jnp.where(up, team + step, team - step) * TEAM + seat)

    after = place_of(jnp.minimum(me + 1, count - 1))
    before = place_of(jnp.maximum(me - 1, 0))
    barrier = pltpu.get_barrier_semaphore()

    @pl.when(has_after)
    def _():
        pl.semaphore_signal(barrier, inc=1, device_id=after, device_id_type=MESH)

    @pl.when(has_before)
    def _():
        pl.semaphore_signal(barrier, inc=1, device_id=before, device_id_type=MESH)

    for r in range(rounds):
        pl.semaphore_signal(barrier, inc=1, device_id=partner(r), device_id_type=MESH)

    @pl.loop(1, TEAM)
    def _(d):
        pl.semaphore_signal(barrier, inc=1, device_id=place_of(mate(d)), device_id_type=MESH)

    def p_copy(g):
        span = pl.ds(g * GROUP, GROUP)
        return pltpu.make_async_copy(p_hbm.at[span], p_v.at[span], p_sem.at[g])

    def a_copy(g):
        span = pl.ds(g * GROUP, GROUP)
        return pltpu.make_async_copy(a_hbm.at[span], a_v.at[span], a_sem.at[g])

    index_copies = [
        pltpu.make_async_copy(source, landing, index_sem.at[k])
        for k, (source, landing) in enumerate(
            (
                (pattern_hbm, pattern),
                (aggregate_hbm, aggregate),
                (owners_hbm, owners),
                (cols_hbm, cols),
            )
        )
    ]
    for copy in index_copies:
        copy.start()
    ends = (0, 1, groups - 2, groups - 1)
    middle = tuple(range(2, groups - 2))
    inner = tuple(range(3, groups - 3))
    for g in ends:
        p_copy(g).start()

    left = lax.broadcasted_iota(jnp.int32, (nodes, 128), 1) < 64
    lane = lax.broadcasted_iota(jnp.int32, (1, 128), 1) < 64

    def place_group(g, at_end):
        for j in range(GROUP):
            i = g * GROUP + j
            second = jnp.where(aggregate[0, i] - me * LW == 1, 1.0, 0.0)
            has0 = pattern[0, i].astype(F32)
            has2 = pattern[2, i].astype(F32)
            x0 = p_v[i, :, :128]
            x2 = p_v[i, :, 128:]
            swapped = jnp.concatenate([x0[:, 64:], x0[:, :64]], axis=1)
            mixed = jnp.concatenate([x2, x0[:, 64:]], axis=1)
            one = jnp.where(lane, second, second * has0).astype(BF16)
            two = jnp.where(lane, (1.0 - second) * has2, 1.0 - second).astype(BF16)
            pooled[HR + i, :, :128] = swapped * one + mixed * two
            if at_end:
                three = jnp.where(lane, (1.0 - second) * has0, second * has2).astype(BF16)
                pooled[HR + i, :, 128:] = jnp.concatenate([x0[:, :64], x2], axis=1) * three
            else:
                pooled[HR + i, :, 128:] = jnp.zeros_like(x0)

    for copy in index_copies:
        copy.wait()

    total_agg = owners.shape[1]
    down = lax.broadcasted_iota(jnp.int32, (total_agg, total_agg), 0)
    over = lax.broadcasted_iota(jnp.int32, (total_agg, total_agg), 1)
    owner_row = owners[...]
    owner_col = jnp.sum(jnp.where(down == over, owner_row, 0), axis=1, keepdims=True)
    rank = jnp.sum(jnp.where((owner_col == owner_row) & (over < down), 1, 0), axis=1, keepdims=True)
    wanted = lax.broadcasted_iota(jnp.int32, (total_agg, 128), 1) + team * (TEAM * OWNMAX)
    number = lax.broadcasted_iota(jnp.int32, (total_agg, 128), 0) + 1
    hit = (owner_col * OWNMAX + rank) == wanted
    found = jnp.sum(jnp.where(hit, number, 0), axis=0, keepdims=True)
    table_v[...] = jnp.broadcast_to(found, table_v.shape)
    table_copy = pltpu.make_async_copy(table_v, table, index_sem.at[4])
    table_copy.start()

    for g in ends:
        p_copy(g).wait()
    for g in middle:
        p_copy(g).start()
    for g in inner + (2, groups - 3, 0, groups - 1, 1, groups - 2):
        a_copy(g).start()

    @pl.loop(0, 2)
    def _(end):
        place_group(end * (groups - 1), True)

    @pl.loop(0, HR // 2)
    def _(i):
        for side, first in ((0, rows - HR), (1, 0)):
            packed[side, i] = jnp.concatenate(
                [p_v[first + i + k, :, 64:128] for k in (0, HR // 2)], axis=1
            )

    @pl.loop(0, SPR // 2)
    def _(i):
        for side, first, at in ((0, HR + rows - SPR, 192), (1, HR, 128)):
            packed_side[side, i] = jnp.concatenate(
                [pooled[first + i + k, :, at : at + 64] for k in (0, SPR // 2)], axis=1
            )

    near = TEAM - 1 + rounds + jnp.where(has_after, 1, 0) + jnp.where(has_before, 1, 0)
    pl.semaphore_wait(barrier, near)

    def rim_copies(side):
        pairs = ((packed.at[side], rim.at[side]), (packed_side.at[side], rim_side.at[side]))
        return [
            pltpu.make_async_remote_copy(
                src_ref=source,
                dst_ref=landing,
                send_sem=rim_send.at[side, half],
                recv_sem=rim_recv.at[side, half],
                device_id=(after, before)[side],
                device_id_type=MESH,
            )
            for half, (source, landing) in enumerate(pairs)
        ]

    sends = (has_after, has_before)
    receives = (has_before, has_after)
    rims = [rim_copies(side) for side in range(2)]
    for side in range(2):
        @pl.when(sends[side])
        def _():
            for copy in rims[side]:
                copy.start()

    def vouch_for(r):
        pl.semaphore_signal(vouch.at[r], inc=1, device_id=partner(r), device_id_type=MESH)

    vouch_for(0)

    @pl.loop(0, 2)
    def _(end):
        place_group(1 + end * (groups - 3), False)

    @pl.loop(2, groups - 2)
    def _(g):
        p_copy(g).wait()
        place_group(g, False)

    @pl.loop(0, HR)
    def _(i):
        pooled[i] = jnp.zeros((nodes, 256), BF16)
        pooled[rows + HR + i] = jnp.zeros((nodes, 256), BF16)

    sums[...] = jnp.zeros_like(sums)
    base = HR - me * rows

    def apply_rows(first, total, buffer, width):
        for j in range(total):
            i = first + j
            stack = jnp.concatenate(
                [pooled[jnp.maximum(cols[k, i] + base, 0), :, :width] for k in range(8)], axis=0
            )
            product = jnp.dot(a_v[i], stack, preferred_element_type=F32)
            applied[buffer, j * nodes : (j + 1) * nodes, :width] = product.astype(BF16)

    def add_up(first, total, buffer, high, width):
        left_rows = pooled[pl.ds(HR + first, total), :, :high].reshape(total * nodes, high)
        sums[:high, :width] += lax.dot_general(
            left_rows, applied[buffer, : total * nodes, :width], (((0,), (0,)), ((), ())),
            preferred_element_type=F32,
        )

    def run_pair(first, later, total, high, width):
        apply_rows(first, total, 0, width)
        apply_rows(later, total, 1, width)
        add_up(first, total, 0, high, width)
        add_up(later, total, 1, high, width)

    @pl.loop(0, len(inner) // 2)
    def _(step):
        g = inner[0] + 2 * step
        a_copy(g).wait()
        a_copy(g + 1).wait()
        run_pair(g * GROUP, (g + 1) * GROUP, GROUP, 128, 128)

    pl.semaphore_wait(vouch.at[0], 1)
    for r in range(1, rounds):
        vouch_for(r)
        if r < rounds - 1:
            pl.semaphore_wait(vouch.at[r], 1)

    a_copy(2).wait()
    a_copy(groups - 3).wait()
    run_pair(2 * GROUP, (groups - 3) * GROUP, GROUP, 128, 256)
    for g in ends:
        a_copy(g).wait()

    zero = jnp.zeros((nodes, 128), BF16)
    for side, first in enumerate((0, rows + HR)):
        @pl.when(receives[side])
        def _():
            for copy in rims[side]:
                copy.wait_recv()
            keep = left if side == 0 else ~left

            @pl.loop(0, HR // 2, unroll=4)
            def _(i):
                both = rim[side, i]
                swapped = jnp.concatenate([both[:, 64:], both[:, :64]], axis=1)
                early, late = (both, swapped) if side == 0 else (swapped, both)
                for k, own in ((0, early), (HR // 2, late)):
                    pooled[first + i + k, :, 128:] = jnp.where(keep, own, zero)

            start = HR - SPR if side == 0 else rows + HR

            @pl.loop(0, SPR // 2, unroll=2)
            def _(i):
                both = rim_side[side, i]
                swapped = jnp.concatenate([both[:, 64:], both[:, :64]], axis=1)
                early, late = (swapped, both) if side == 0 else (both, swapped)
                for k, own in ((0, early), (SPR // 2, late)):
                    pooled[start + i + k, :, :128] = jnp.where(keep, zero, own)

    run_pair(0, rows - SPR, SPR, 256, 256)

    edge_out[0, :, :64] = sums[192:, :64]
    edge_out[0, :, 64:] = sums[192:, 192:]
    edge_out[1, :, :64] = sums[128:192, 128:192]
    edge_out[1, :, 64:] = sums[128:192, 64:128]
    edges = [
        pltpu.make_async_remote_copy(
            src_ref=edge_out.at[side],
            dst_ref=edge_in.at[side],
            send_sem=edge_send.at[side],
            recv_sem=edge_recv.at[side],
            device_id=(after, before)[side],
            device_id_type=MESH,
        )
        for side in range(2)
    ]
    for side in range(2):
        @pl.when(sends[side])
        def _():
            edges[side].start()

    @pl.loop(0, 2)
    def _(side):
        first = SPR + side * (rows - HR - SPR)
        apply_rows(first, HR - SPR, 0, 256)
        add_up(first, HR - SPR, 0, 128, 256)

    table_copy.wait()
    if rounds:
        pl.semaphore_wait(vouch.at[rounds - 1], 1)
    for side in range(2):
        @pl.when(receives[side])
        def _():
            edges[side].wait_recv()

        @pl.when(~receives[side])
        def _():
            edge_in[side] = jnp.zeros((nodes, 128), F32)

    early, late = edge_in[0], edge_in[1]
    front0 = jnp.concatenate([sums[64:128, 128:192], sums[64:128, 64:128]], axis=1) + early
    front1 = jnp.concatenate([sums[:64, 64:128], sums[:64, :64] + late[:, :64]], axis=1)
    tails = jnp.concatenate([sums[64:128, :64], sums[:64, 192:] + late[:, 64:]], axis=1)
    lines = nodes // TEAM
    for s in range(TEAM):
        part = slice(s * lines, (s + 1) * lines)
        piece_out[s, : 2 * lines] = jnp.concatenate([front0[part], front1[part]], axis=0).astype(BF16)
        piece_out[s, 2 * lines :] = tails[part].astype(BF16)

    def piece_copy(d):
        there = lax.rem(me + d, count)
        return pltpu.make_async_remote_copy(
            src_ref=piece_out.at[lax.rem(there, TEAM)],
            dst_ref=spread.at[me],
            send_sem=piece_send.at[d],
            recv_sem=piece_recv.at[d],
            device_id=place_of(there),
            device_id_type=MESH,
        )

    @pl.loop(1, count)
    def _(d):
        piece_copy(d).start()

    spread[me] = piece_out[seat]

    @pl.loop(1, count)
    def _(d):
        piece_copy(d).wait_recv()

    low = lax.broadcasted_iota(jnp.int32, (lines, 128), 1) < 64

    def fill(there, box):
        fronts, ends_of = [], []
        for s in range(OWNMAX):
            entry = table[0, there * OWNMAX + s]
            agg = jnp.maximum(entry - 1, 0)
            which = lax.rem(agg, LW)
            piece = spread[agg // LW].astype(F32)
            front = jnp.where(which == 1, piece[lines : 2 * lines], piece[:lines])
            fronts.append(jnp.where(entry > 0, front, 0.0))
            tail = piece[2 * lines :]
            swapped = jnp.concatenate([tail[:, 64:], tail[:, :64]], axis=1)
            tail = jnp.where(which == s % 2, tail, swapped)
            ends_of.append(jnp.where(entry > 0, tail, 0.0))
        for k in range(OWNMAX // 2):
            box[k] = jnp.concatenate(fronts[2 * k : 2 * k + 2], axis=0).astype(BF16)
        tails = [jnp.where(low, ends_of[2 * k], ends_of[2 * k + 1]) for k in range(OWNMAX // 2)]
        for k in range(OWNMAX // 4):
            box[OWNMAX // 2 + k] = jnp.concatenate(tails[2 * k : 2 * k + 2], axis=0).astype(BF16)

    def mail_copy(d):
        return pltpu.make_async_remote_copy(
            src_ref=mail_out.at[d],
            dst_ref=mail_in.at[seat],
            send_sem=mail_send.at[d],
            recv_sem=mail_recv.at[d],
            device_id=place_of(mate(d)),
            device_id_type=MESH,
        )

    @pl.loop(1, TEAM)
    def _(d):
        fill(lax.rem(seat + d, TEAM), mail_out.at[d])
        mail_copy(d).start()

    fill(seat, mail_in.at[seat])

    @pl.loop(1, TEAM)
    def _(d):
        mail_copy(d).wait_recv()

    for m in range(TEAM // 2):
        span = pl.ds(2 * lines * m, 2 * lines)
        for k in range(OWNMAX // 2):
            one, two = (mail_in[2 * m + q, k].astype(F32) for q in range(2))
            for h in range(2):
                part = slice(h * lines, (h + 1) * lines)
                out[2 * k + h, span, :128] = jnp.concatenate([one[part], two[part]], axis=0).astype(BF16)
        for k in range(OWNMAX // 4):
            one, two = (mail_in[2 * m + q, OWNMAX // 2 + k].astype(F32) for q in range(2))
            for h in range(2):
                part = slice(h * lines, (h + 1) * lines)
                both = jnp.concatenate([one[part], two[part]], axis=0).astype(BF16)
                out[4 * k + 2 * h, span, 128:] = both[:, :64]
                out[4 * k + 2 * h + 1, span, 128:] = both[:, 64:]

    for side in range(2):
        @pl.when(sends[side])
        def _():
            for copy in rims[side] + [edges[side]]:
                copy.wait_send()

    @pl.loop(1, count)
    def _(d):
        piece_copy(d).wait_send()

    @pl.loop(1, TEAM)
    def _(d):
        mail_copy(d).wait_send()


def shards(a_blocks, a_columns, p_blocks, p_pattern, aggregate, owner_map):
    rows, nodes = a_blocks.shape[:2]
    count = lax.axis_size(AXES)
    vmem = pl.BlockSpec(memory_space=pltpu.VMEM)
    hbm = pl.BlockSpec(memory_space=pl.ANY)
    groups = rows // GROUP
    lines = nodes // TEAM
    half = OWNMAX // 2 + OWNMAX // 4
    dma = pltpu.SemaphoreType.DMA
    pool = (rows + 2 * HR, nodes, 4 * nodes)
    total_agg = owner_map.shape[0]
    return pl.pallas_call(
        kernel,
        out_shape=jax.ShapeDtypeStruct((OWNMAX, nodes, 3 * nodes), BF16),
        in_specs=[hbm] * 6,
        out_specs=vmem,
        scratch_shapes=[
            pltpu.SMEM((a_columns.shape[1], rows), jnp.int32),
            pltpu.SMEM((3, rows), jnp.int32),
            pltpu.SMEM((1, rows), jnp.int32),
            pltpu.VMEM((1, total_agg), jnp.int32),
            pltpu.VMEM(a_blocks.shape, BF16),
            pltpu.VMEM(p_blocks.shape, BF16),
            pltpu.VMEM(pool, BF16),
            pltpu.VMEM((2, (HR - SPR) * nodes, 4 * nodes), BF16),
            pltpu.VMEM((4 * nodes, 4 * nodes), F32),
            pltpu.VMEM((2, HR // 2, nodes, 2 * nodes), BF16),
            pltpu.VMEM((2, SPR // 2, nodes, 2 * nodes), BF16),
            pltpu.VMEM((2, HR // 2, nodes, 2 * nodes), BF16),
            pltpu.VMEM((2, SPR // 2, nodes, 2 * nodes), BF16),
            pltpu.VMEM((2, nodes, 2 * nodes), F32),
            pltpu.VMEM((2, nodes, 2 * nodes), F32),
            pltpu.VMEM((TEAM, 3 * lines, 128), BF16),
            pltpu.VMEM((count, 3 * lines, 128), BF16),
            pltpu.VMEM((TEAM, half, 2 * lines, 128), BF16),
            pltpu.VMEM((TEAM, half, 2 * lines, 128), BF16),
            pltpu.VMEM((8, 128), jnp.int32),
            pltpu.SMEM((8, 128), jnp.int32),
            dma((groups,)),
            dma((groups,)),
            dma((5,)),
            dma((2, 2)),
            dma((2, 2)),
            dma((2,)),
            dma((2,)),
            dma((count,)),
            dma((count,)),
            dma((TEAM,)),
            dma((TEAM,)),
            pltpu.SemaphoreType.REGULAR((max(count // TEAM - 1, 1).bit_length(),)),
        ],
        compiler_params=pltpu.CompilerParams(
            collective_id=0, has_side_effects=True, vmem_limit_bytes=56 << 20
        ),
    )(a_blocks, a_columns.T, p_blocks, p_pattern.T, aggregate[None], owner_map[None])


def solution(mesh):
    placed = (
        P(AXES, None, None),
        P(AXES, None),
        P(AXES, None, None),
        P(AXES, None),
        P(AXES),
        P(),
    )
    return jax.shard_map(
        shards,
        mesh=mesh,
        in_specs=placed,
        out_specs=P(AXES, None, None),
        check_vma=False,
    )
```

```python
import jax
import jax.numpy as jnp
from jax import lax
from jax.experimental import pallas as pl
from jax.experimental.pallas import tpu as pltpu
from jax.sharding import PartitionSpec as P

HR = 32
LW = 2
OWNMAX = 8
GROUP = 16
SPR = 8
TEAM = 8
AXES = ("wide", "narrow")
MESH = pl.DeviceIdType.MESH
BF16 = jnp.bfloat16
F32 = jnp.float32


def kernel(a_hbm, cols_hbm, p_hbm, pattern_hbm, aggregate_hbm, owners_hbm, out,
           cols, pattern, aggregate, owners, a_v, p_v, pooled, applied, sums, packed, rim,
           edge_out, edge_in, piece_out, spread, mail_out, mail_in, table_v, table,
           a_sem, p_sem, index_sem, rim_send, rim_recv, edge_send, edge_recv,
           piece_send, piece_recv, mail_send, mail_recv, vouch):
    rows, nodes = a_hbm.shape[0], a_hbm.shape[1]
    me = lax.axis_index(AXES)
    narrow = lax.axis_size("narrow")
    count = lax.axis_size(AXES)
    teams = count // TEAM
    rounds = teams.bit_length() - 1
    team, seat = me // TEAM, lax.rem(me, TEAM)
    groups = rows // GROUP
    has_before, has_after = me > 0, me < count - 1

    def place_of(device):
        return (device // narrow, lax.rem(device, narrow))

    def mate(d):
        return team * TEAM + lax.rem(seat + d, TEAM)

    def partner(r):
        step = 1 << r
        up = lax.rem(team // step, 2) == 0
        return place_of(jnp.where(up, team + step, team - step) * TEAM + seat)

    after = place_of(jnp.minimum(me + 1, count - 1))
    before = place_of(jnp.maximum(me - 1, 0))
    barrier = pltpu.get_barrier_semaphore()

    @pl.when(has_after)
    def _():
        pl.semaphore_signal(barrier, inc=1, device_id=after, device_id_type=MESH)

    @pl.when(has_before)
    def _():
        pl.semaphore_signal(barrier, inc=1, device_id=before, device_id_type=MESH)

    for r in range(rounds):
        pl.semaphore_signal(barrier, inc=1, device_id=partner(r), device_id_type=MESH)

    @pl.loop(1, TEAM)
    def _(d):
        pl.semaphore_signal(barrier, inc=1, device_id=place_of(mate(d)), device_id_type=MESH)

    step = 2 * GROUP

    def p_copy(k):
        first = (0, rows - step, step, rows // 2)[k]
        span = pl.ds(first, step if k < 2 else rows // 2 - step)
        return pltpu.make_async_copy(p_hbm.at[span], p_v.at[span], p_sem.at[k])

    wing = rows // 4
    inner = (rows - 2 * wing) // step

    def a_copy(first, total, k):
        span = pl.ds(first, total)
        return pltpu.make_async_copy(a_hbm.at[span], a_v.at[span], a_sem.at[k])

    def a_inner(k):
        return a_copy(wing + k * step, step, k)

    a_wings = [a_copy(first, wing, inner + k) for k, first in enumerate((0, rows - wing))]

    index_copies = [
        pltpu.make_async_copy(source, landing, index_sem.at[k])
        for k, (source, landing) in enumerate(
            (
                (pattern_hbm, pattern),
                (aggregate_hbm, aggregate),
                (owners_hbm, owners),
                (cols_hbm, cols),
            )
        )
    ]
    for copy in index_copies:
        copy.start()
    for k in range(2):
        p_copy(k).start()

    left = lax.broadcasted_iota(jnp.int32, (nodes, 128), 1) < 64
    lane = lax.broadcasted_iota(jnp.int32, (1, 128), 1) < 64

    def place_group(g, at_end):
        for j in range(GROUP):
            i = g * GROUP + j
            second = jnp.where(aggregate[0, i] - me * LW == 1, 1.0, 0.0)
            has0 = pattern[0, i].astype(F32)
            has2 = pattern[2, i].astype(F32)
            x0 = p_v[i, :, :128]
            x2 = p_v[i, :, 128:]
            swapped = jnp.concatenate([x0[:, 64:], x0[:, :64]], axis=1)
            mixed = jnp.concatenate([x2, x0[:, 64:]], axis=1)
            one = jnp.where(lane, second, second * has0).astype(BF16)
            two = jnp.where(lane, (1.0 - second) * has2, 1.0 - second).astype(BF16)
            pooled[HR + i, :, :128] = swapped * one + mixed * two
            if at_end:
                three = jnp.where(lane, (1.0 - second) * has0, second * has2).astype(BF16)
                pooled[HR + i, :, 128:] = jnp.concatenate([x0[:, :64], x2], axis=1) * three
            else:
                pooled[HR + i, :, 128:] = jnp.zeros_like(x0)

    for copy in index_copies:
        copy.wait()

    total_agg = owners.shape[1]
    down = lax.broadcasted_iota(jnp.int32, (total_agg, total_agg), 0)
    over = lax.broadcasted_iota(jnp.int32, (total_agg, total_agg), 1)
    owner_row = owners[...]
    owner_col = jnp.sum(jnp.where(down == over, owner_row, 0), axis=1, keepdims=True)
    rank = jnp.sum(jnp.where((owner_col == owner_row) & (over < down), 1, 0), axis=1, keepdims=True)
    wanted = lax.broadcasted_iota(jnp.int32, (total_agg, 128), 1) + team * (TEAM * OWNMAX)
    number = lax.broadcasted_iota(jnp.int32, (total_agg, 128), 0) + 1
    hit = (owner_col * OWNMAX + rank) == wanted
    found = jnp.sum(jnp.where(hit, number, 0), axis=0, keepdims=True)
    table_v[...] = jnp.broadcast_to(found, table_v.shape)
    table_copy = pltpu.make_async_copy(table_v, table, index_sem.at[4])
    table_copy.start()

    for k in range(2):
        p_copy(k).wait()
    for k in range(2, 4):
        p_copy(k).start()
    for k in range(inner):
        a_inner(k).start()
    for copy in a_wings:
        copy.start()

    @pl.loop(0, 2)
    def _(end):
        place_group(end * (groups - 1), True)

    @pl.loop(0, HR // 2)
    def _(i):
        for side, first in ((0, rows - HR), (1, 0)):
            packed[side, i] = jnp.concatenate(
                [p_v[first + i + k, :, 64:128] for k in (0, HR // 2)], axis=1
            )

    @pl.loop(0, SPR // 2)
    def _(i):
        for side, first, at in ((0, HR + rows - SPR, 192), (1, HR, 128)):
            packed[side, HR // 2 + i] = jnp.concatenate(
                [pooled[first + i + k, :, at : at + 64] for k in (0, SPR // 2)], axis=1
            )

    @pl.loop(0, 2)
    def _(end):
        place_group(1 + end * (groups - 3), False)

    @pl.loop(0, HR)
    def _(i):
        pooled[i] = jnp.zeros((nodes, 256), BF16)
        pooled[rows + HR + i] = jnp.zeros((nodes, 256), BF16)

    sums[...] = jnp.zeros_like(sums)
    near = TEAM - 1 + rounds + jnp.where(has_after, 1, 0) + jnp.where(has_before, 1, 0)
    pl.semaphore_wait(barrier, near)

    def both_ways(outbox, inbox, send_sem, recv_sem):
        return [
            pltpu.make_async_remote_copy(
                src_ref=outbox.at[side],
                dst_ref=inbox.at[side],
                send_sem=send_sem.at[side],
                recv_sem=recv_sem.at[side],
                device_id=(after, before)[side],
                device_id_type=MESH,
            )
            for side in range(2)
        ]

    sends = (has_after, has_before)
    receives = (has_before, has_after)
    rims = both_ways(packed, rim, rim_send, rim_recv)
    for side in range(2):
        @pl.when(sends[side])
        def _():
            rims[side].start()

    def vouch_for(r):
        pl.semaphore_signal(vouch.at[r], inc=1, device_id=partner(r), device_id_type=MESH)

    vouch_for(0)
    for k in range(2, 4):
        p_copy(k).wait()

    @pl.loop(2, groups - 2)
    def _(g):
        place_group(g, False)

    base = HR - me * rows

    def apply_rows(first, total, buffer, width):
        for j in range(total):
            i = first + j
            stack = jnp.concatenate(
                [pooled[jnp.maximum(cols[k, i] + base, 0), :, :width] for k in range(8)], axis=0
            )
            product = jnp.dot(a_v[i], stack, preferred_element_type=F32)
            applied[buffer, j * nodes : (j + 1) * nodes, :width] = product.astype(BF16)

    def add_up(first, total, buffer, high, width):
        left_rows = pooled[pl.ds(HR + first, total), :, :high].reshape(total * nodes, high)
        sums[:high, :width] += lax.dot_general(
            left_rows, applied[buffer, : total * nodes, :width], (((0,), (0,)), ((), ())),
            preferred_element_type=F32,
        )

    def run_pair(first, later, total, high, width):
        apply_rows(first, total, 0, width)
        apply_rows(later, total, 1, width)
        add_up(first, total, 0, high, width)
        add_up(later, total, 1, high, width)

    @pl.loop(0, inner)
    def _(k):
        a_inner(k).wait()
        first = wing + k * step
        run_pair(first, first + GROUP, GROUP, 128, 128)

    pl.semaphore_wait(vouch.at[0], 1)
    for r in range(1, rounds):
        vouch_for(r)
        if r < rounds - 1:
            pl.semaphore_wait(vouch.at[r], 1)
    for copy in a_wings:
        copy.wait()
    run_pair(HR, rows - HR - GROUP, GROUP, 128, 256)

    zero = jnp.zeros((nodes, 128), BF16)
    for side, first in enumerate((0, rows + HR)):
        @pl.when(receives[side])
        def _():
            rims[side].wait_recv()
            keep = left if side == 0 else ~left

            @pl.loop(0, HR // 2, unroll=4)
            def _(i):
                both = rim[side, i]
                swapped = jnp.concatenate([both[:, 64:], both[:, :64]], axis=1)
                early, late = (both, swapped) if side == 0 else (swapped, both)
                for k, own in ((0, early), (HR // 2, late)):
                    pooled[first + i + k, :, 128:] = jnp.where(keep, own, zero)

            start = HR - SPR if side == 0 else rows + HR

            @pl.loop(0, SPR // 2, unroll=2)
            def _(i):
                both = rim[side, HR // 2 + i]
                swapped = jnp.concatenate([both[:, 64:], both[:, :64]], axis=1)
                early, late = (swapped, both) if side == 0 else (both, swapped)
                for k, own in ((0, early), (SPR // 2, late)):
                    pooled[start + i + k, :, :128] = jnp.where(keep, zero, own)

    run_pair(0, rows - SPR, SPR, 256, 256)

    edge_out[0, :, :64] = sums[192:, :64]
    edge_out[0, :, 64:] = sums[192:, 192:]
    edge_out[1, :, :64] = sums[128:192, 128:192]
    edge_out[1, :, 64:] = sums[128:192, 64:128]
    edges = both_ways(edge_out, edge_in, edge_send, edge_recv)
    for side in range(2):
        @pl.when(sends[side])
        def _():
            edges[side].start()

    @pl.loop(0, 2)
    def _(side):
        first = SPR + side * (rows - HR - SPR)
        apply_rows(first, HR - SPR, 0, 256)
        add_up(first, HR - SPR, 0, 128, 256)

    table_copy.wait()
    if rounds:
        pl.semaphore_wait(vouch.at[rounds - 1], 1)
    for side in range(2):
        @pl.when(receives[side])
        def _():
            edges[side].wait_recv()

        @pl.when(~receives[side])
        def _():
            edge_in[side] = jnp.zeros((nodes, 128), F32)

    early, late = edge_in[0], edge_in[1]
    front0 = jnp.concatenate([sums[64:128, 128:192], sums[64:128, 64:128]], axis=1) + early
    front1 = jnp.concatenate([sums[:64, 64:128], sums[:64, :64] + late[:, :64]], axis=1)
    tails = jnp.concatenate([sums[64:128, :64], sums[:64, 192:] + late[:, 64:]], axis=1)
    lines = nodes // TEAM
    for s in range(TEAM):
        part = slice(s * lines, (s + 1) * lines)
        piece_out[s, : 2 * lines] = jnp.concatenate([front0[part], front1[part]], axis=0).astype(BF16)
        piece_out[s, 2 * lines :] = tails[part].astype(BF16)

    def piece_copy(d):
        there = lax.rem(me + d, count)
        return pltpu.make_async_remote_copy(
            src_ref=piece_out.at[lax.rem(there, TEAM)],
            dst_ref=spread.at[me],
            send_sem=piece_send,
            recv_sem=piece_recv,
            device_id=place_of(there),
            device_id_type=MESH,
        )

    @pl.loop(1, count)
    def _(d):
        piece_copy(d).start()

    spread[me] = piece_out[seat]

    others = spread.at[pl.ds(0, count - 1)]
    all_pieces = pltpu.make_async_remote_copy(
        src_ref=others, dst_ref=others, send_sem=piece_send, recv_sem=piece_recv,
        device_id=after, device_id_type=MESH,
    )
    all_pieces.wait_recv()

    low = lax.broadcasted_iota(jnp.int32, (lines, 128), 1) < 64

    def fill(there, box):
        fronts, ends_of = [], []
        for s in range(OWNMAX):
            entry = table[0, there * OWNMAX + s]
            agg = jnp.maximum(entry - 1, 0)
            which = lax.rem(agg, LW)
            piece = spread[agg // LW].astype(F32)
            front = jnp.where(which == 1, piece[lines : 2 * lines], piece[:lines])
            fronts.append(jnp.where(entry > 0, front, 0.0))
            tail = piece[2 * lines :]
            swapped = jnp.concatenate([tail[:, 64:], tail[:, :64]], axis=1)
            tail = jnp.where(which == s % 2, tail, swapped)
            ends_of.append(jnp.where(entry > 0, tail, 0.0))
        for k in range(OWNMAX // 2):
            box[k] = jnp.concatenate(fronts[2 * k : 2 * k + 2], axis=0).astype(BF16)
        tails = [jnp.where(low, ends_of[2 * k], ends_of[2 * k + 1]) for k in range(OWNMAX // 2)]
        for k in range(OWNMAX // 4):
            box[OWNMAX // 2 + k] = jnp.concatenate(tails[2 * k : 2 * k + 2], axis=0).astype(BF16)

    def mail_copy(d):
        return pltpu.make_async_remote_copy(
            src_ref=mail_out.at[d],
            dst_ref=mail_in.at[seat],
            send_sem=mail_send,
            recv_sem=mail_recv,
            device_id=place_of(mate(d)),
            device_id_type=MESH,
        )

    @pl.loop(1, TEAM)
    def _(d):
        fill(lax.rem(seat + d, TEAM), mail_out.at[d])
        mail_copy(d).start()

    fill(seat, mail_in.at[seat])

    boxes = mail_in.at[pl.ds(0, TEAM - 1)]
    all_mail = pltpu.make_async_remote_copy(
        src_ref=boxes, dst_ref=boxes, send_sem=mail_send, recv_sem=mail_recv,
        device_id=after, device_id_type=MESH,
    )
    all_mail.wait_recv()

    for m in range(TEAM // 2):
        span = pl.ds(2 * lines * m, 2 * lines)
        for k in range(OWNMAX // 2):
            one, two = (mail_in[2 * m + q, k].astype(F32) for q in range(2))
            for h in range(2):
                part = slice(h * lines, (h + 1) * lines)
                out[2 * k + h, span, :128] = jnp.concatenate([one[part], two[part]], axis=0).astype(BF16)
        for k in range(OWNMAX // 4):
            one, two = (mail_in[2 * m + q, OWNMAX // 2 + k].astype(F32) for q in range(2))
            for h in range(2):
                part = slice(h * lines, (h + 1) * lines)
                both = jnp.concatenate([one[part], two[part]], axis=0).astype(BF16)
                out[4 * k + 2 * h, span, 128:] = both[:, :64]
                out[4 * k + 2 * h + 1, span, 128:] = both[:, 64:]

    for side in range(2):
        @pl.when(sends[side])
        def _():
            rims[side].wait_send()
            edges[side].wait_send()

    all_pieces.wait_send()

    all_mail.wait_send()


def shards(a_blocks, a_columns, p_blocks, p_pattern, aggregate, owner_map):
    rows, nodes = a_blocks.shape[:2]
    count = lax.axis_size(AXES)
    vmem = pl.BlockSpec(memory_space=pltpu.VMEM)
    hbm = pl.BlockSpec(memory_space=pl.ANY)
    lines = nodes // TEAM
    half = OWNMAX // 2 + OWNMAX // 4
    dma = pltpu.SemaphoreType.DMA
    pool = (rows + 2 * HR, nodes, 4 * nodes)
    total_agg = owner_map.shape[0]
    return pl.pallas_call(
        kernel,
        out_shape=jax.ShapeDtypeStruct((OWNMAX, nodes, 3 * nodes), BF16),
        in_specs=[hbm] * 6,
        out_specs=vmem,
        scratch_shapes=[
            pltpu.SMEM((a_columns.shape[1], rows), jnp.int32),
            pltpu.SMEM((3, rows), jnp.int32),
            pltpu.SMEM((1, rows), jnp.int32),
            pltpu.VMEM((1, total_agg), jnp.int32),
            pltpu.VMEM(a_blocks.shape, BF16),
            pltpu.VMEM(p_blocks.shape, BF16),
            pltpu.VMEM(pool, BF16),
            pltpu.VMEM((2, (HR - SPR) * nodes, 4 * nodes), BF16),
            pltpu.VMEM((4 * nodes, 4 * nodes), F32),
            pltpu.VMEM((2, (HR + SPR) // 2, nodes, 2 * nodes), BF16),
            pltpu.VMEM((2, (HR + SPR) // 2, nodes, 2 * nodes), BF16),
            pltpu.VMEM((2, nodes, 2 * nodes), F32),
            pltpu.VMEM((2, nodes, 2 * nodes), F32),
            pltpu.VMEM((TEAM, 3 * lines, 128), BF16),
            pltpu.VMEM((count, 3 * lines, 128), BF16),
            pltpu.VMEM((TEAM, half, 2 * lines, 128), BF16),
            pltpu.VMEM((TEAM, half, 2 * lines, 128), BF16),
            pltpu.VMEM((8, 128), jnp.int32),
            pltpu.SMEM((8, 128), jnp.int32),
            dma((rows // 4 // GROUP + 2,)),
            dma((4,)),
            dma((5,)),
            dma((2,)),
            dma((2,)),
            dma((2,)),
            dma((2,)),
            dma,
            dma,
            dma,
            dma,
            pltpu.SemaphoreType.REGULAR((max(count // TEAM - 1, 1).bit_length(),)),
        ],
        compiler_params=pltpu.CompilerParams(
            collective_id=0, has_side_effects=True, vmem_limit_bytes=56 << 20
        ),
    )(a_blocks, a_columns.T, p_blocks, p_pattern.T, aggregate[None], owner_map[None])


def solution(mesh):
    placed = (
        P(AXES, None, None),
        P(AXES, None),
        P(AXES, None, None),
        P(AXES, None),
        P(AXES),
        P(),
    )
    return jax.shard_map(
        shards,
        mesh=mesh,
        in_specs=placed,
        out_specs=P(AXES, None, None),
        check_vma=False,
    )
```

```python
import jax
import jax.numpy as jnp
from jax import lax
from jax.experimental import pallas as pl
from jax.experimental.pallas import tpu as pltpu
from jax.sharding import PartitionSpec as P

HR = 32
LW = 2
OWNMAX = 8
GROUP = 16
SPR = 8
TEAM = 8
AXES = ("wide", "narrow")
MESH = pl.DeviceIdType.MESH
BF16 = jnp.bfloat16
F32 = jnp.float32


def kernel(a_hbm, cols_hbm, p_hbm, pattern_hbm, aggregate_hbm, owners_hbm, out,
           cols, pattern, aggregate, owners, a_v, p_v, pooled, applied, sums, packed, packed_side, rim, rim_side,
           edge_out, edge_in, piece_out, spread, mail_out, mail_in, table_v, table,
           a_sem, p_sem, index_sem, rim_send, rim_recv, spill_send, spill_recv, edge_send, edge_recv,
           piece_send, piece_recv, mail_send, mail_recv, vouch):
    rows, nodes = a_hbm.shape[0], a_hbm.shape[1]
    me = lax.axis_index(AXES)
    narrow = lax.axis_size("narrow")
    count = lax.axis_size(AXES)
    teams = count // TEAM
    rounds = teams.bit_length() - 1
    team, seat = me // TEAM, lax.rem(me, TEAM)
    groups = rows // GROUP
    has_before, has_after = me > 0, me < count - 1

    def place_of(device):
        return (device // narrow, lax.rem(device, narrow))

    def mate(d):
        return team * TEAM + lax.rem(seat + d, TEAM)

    def partner(r):
        step = TEAM << r
        up = lax.rem(me // step, 2) == 0
        return place_of(jnp.where(up, me + step, me - step))

    after = place_of(jnp.minimum(me + 1, count - 1))
    before = place_of(jnp.maximum(me - 1, 0))
    barrier = pltpu.get_barrier_semaphore()

    @pl.when(has_after)
    def _():
        pl.semaphore_signal(barrier, inc=1, device_id=after, device_id_type=MESH)

    @pl.when(has_before)
    def _():
        pl.semaphore_signal(barrier, inc=1, device_id=before, device_id_type=MESH)

    @pl.loop(1, TEAM)
    def _(d):
        pl.semaphore_signal(barrier, inc=1, device_id=place_of(mate(d)), device_id_type=MESH)

    for r in range(rounds):
        pl.semaphore_signal(barrier, inc=1, device_id=partner(r), device_id_type=MESH)

    step = 2 * GROUP

    def p_copy(k):
        first = (0, rows - step, step, rows // 2)[k]
        span = pl.ds(first, step if k < 2 else rows // 2 - step)
        return pltpu.make_async_copy(p_hbm.at[span], p_v.at[span], p_sem.at[k])

    wing = rows // 4
    inner = (rows - 2 * wing) // step

    def a_copy(first, total, k):
        span = pl.ds(first, total)
        return pltpu.make_async_copy(a_hbm.at[span], a_v.at[span], a_sem.at[k])

    def a_inner(k):
        return a_copy(wing + k * step, step, k)

    a_wings = [a_copy(first, wing, inner + k) for k, first in enumerate((0, rows - wing))]

    for k in range(2):
        p_copy(k).start()
    index_copies = [
        pltpu.make_async_copy(source, landing, index_sem.at[k])
        for k, (source, landing) in enumerate(
            (
                (pattern_hbm, pattern),
                (aggregate_hbm, aggregate),
                (owners_hbm, owners),
                (cols_hbm, cols),
            )
        )
    ]
    for copy in index_copies:
        copy.start()

    left = lax.broadcasted_iota(jnp.int32, (nodes, 128), 1) < 64
    lane = lax.broadcasted_iota(jnp.int32, (1, 128), 1) < 64

    def place_group(g, at_end):
        for j in range(GROUP):
            i = g * GROUP + j
            second = jnp.where(aggregate[0, i] - me * LW == 1, 1.0, 0.0)
            has0 = pattern[0, i].astype(F32)
            has2 = pattern[2, i].astype(F32)
            x0 = p_v[i, :, :128]
            x2 = p_v[i, :, 128:]
            swapped = jnp.concatenate([x0[:, 64:], x0[:, :64]], axis=1)
            mixed = jnp.concatenate([x2, x0[:, 64:]], axis=1)
            one = jnp.where(lane, second, second * has0).astype(BF16)
            two = jnp.where(lane, (1.0 - second) * has2, 1.0 - second).astype(BF16)
            pooled[HR + i, :, :128] = swapped * one + mixed * two
            if at_end:
                three = jnp.where(lane, (1.0 - second) * has0, second * has2).astype(BF16)
                pooled[HR + i, :, 128:] = jnp.concatenate([x0[:, :64], x2], axis=1) * three
            else:
                pooled[HR + i, :, 128:] = jnp.zeros_like(x0)

    for k in range(2):
        p_copy(k).wait()
    for k in range(2, 4):
        p_copy(k).start()
    for k in range(inner):
        a_inner(k).start()
    for copy in a_wings:
        copy.start()

    @pl.loop(0, HR // 2, unroll=4)
    def _(i):
        for side, first in ((0, rows - HR), (1, 0)):
            packed[side, i] = jnp.concatenate(
                [p_v[first + i + k, :, 64:128] for k in (0, HR // 2)], axis=1
            )

    near = TEAM - 1 + rounds + jnp.where(has_after, 1, 0) + jnp.where(has_before, 1, 0)
    pl.semaphore_wait(barrier, near)

    def both_ways(outbox, inbox, send_sem, recv_sem):
        return [
            pltpu.make_async_remote_copy(
                src_ref=outbox.at[side],
                dst_ref=inbox.at[side],
                send_sem=send_sem.at[side],
                recv_sem=recv_sem.at[side],
                device_id=(after, before)[side],
                device_id_type=MESH,
            )
            for side in range(2)
        ]

    sends = (has_after, has_before)
    receives = (has_before, has_after)
    def send(copies):
        for side in range(2):
            @pl.when(sends[side])
            def _():
                copies[side].start()

    rims = both_ways(packed, rim, rim_send, rim_recv)
    spills = both_ways(packed_side, rim_side, spill_send, spill_recv)
    send(rims)

    def vouch_for(r):
        pl.semaphore_signal(vouch.at[r], inc=1, device_id=partner(r), device_id_type=MESH)

    def pass_on(r):
        pl.semaphore_wait(vouch.at[r - 1], 1)
        vouch_for(r)

    vouch_for(0)
    for copy in index_copies:
        copy.wait()

    @pl.loop(0, 2)
    def _(end):
        place_group(end * (groups - 1), True)

    @pl.loop(0, SPR // 2, unroll=2)
    def _(i):
        for side, first, at in ((0, HR + rows - SPR, 192), (1, HR, 128)):
            packed_side[side, i] = jnp.concatenate(
                [pooled[first + i + k, :, at : at + 64] for k in (0, SPR // 2)], axis=1
            )

    send(spills)

    total_agg = owners.shape[1]
    down = lax.broadcasted_iota(jnp.int32, (total_agg, total_agg), 0)
    over = lax.broadcasted_iota(jnp.int32, (total_agg, total_agg), 1)
    owner_row = owners[...]
    owner_col = jnp.sum(jnp.where(down == over, owner_row, 0), axis=1, keepdims=True)
    rank = jnp.sum(jnp.where((owner_col == owner_row) & (over < down), 1, 0), axis=1, keepdims=True)
    wanted = lax.broadcasted_iota(jnp.int32, (total_agg, 128), 1) + team * (TEAM * OWNMAX)
    number = lax.broadcasted_iota(jnp.int32, (total_agg, 128), 0) + 1
    hit = (owner_col * OWNMAX + rank) == wanted
    found = jnp.sum(jnp.where(hit, number, 0), axis=0, keepdims=True)
    table_v[...] = jnp.broadcast_to(found, table_v.shape)
    table_copy = pltpu.make_async_copy(table_v, table, index_sem.at[4])
    table_copy.start()

    @pl.loop(0, 2)
    def _(end):
        place_group(1 + end * (groups - 3), False)

    @pl.loop(0, HR)
    def _(i):
        pooled[i] = jnp.zeros((nodes, 256), BF16)
        pooled[rows + HR + i] = jnp.zeros((nodes, 256), BF16)

    sums[...] = jnp.zeros_like(sums)
    for k in range(2, 4):
        p_copy(k).wait()

    @pl.loop(2, groups - 2)
    def _(g):
        place_group(g, False)

    base = HR - me * rows

    def apply_rows(first, total, buffer, width):
        for j in range(total):
            i = first + j
            stack = jnp.concatenate(
                [pooled[jnp.maximum(cols[k, i] + base, 0), :, :width] for k in range(8)], axis=0
            )
            product = jnp.dot(a_v[i], stack, preferred_element_type=F32)
            applied[buffer, j * nodes : (j + 1) * nodes, :width] = product.astype(BF16)

    def add_up(first, total, buffer, high, width):
        left_rows = pooled[pl.ds(HR + first, total), :, :high].reshape(total * nodes, high)
        sums[:high, :width] += lax.dot_general(
            left_rows, applied[buffer, : total * nodes, :width], (((0,), (0,)), ((), ())),
            preferred_element_type=F32,
        )

    def run_pair(first, later, total, high, width):
        apply_rows(first, total, 0, width)
        apply_rows(later, total, 1, width)
        add_up(first, total, 0, high, width)
        add_up(later, total, 1, high, width)

    @pl.loop(0, inner)
    def _(k):
        a_inner(k).wait()
        first = wing + k * step
        run_pair(first, first + GROUP, GROUP, 128, 128)

    for copy in a_wings:
        copy.wait()
    pass_on(1)

    zero = jnp.zeros((nodes, 128), BF16)
    for side, first in enumerate((0, rows + HR)):
        @pl.when(receives[side])
        def _():
            rims[side].wait_recv()
            spills[side].wait_recv()
            keep = left if side == 0 else ~left

            @pl.loop(0, HR // 2, unroll=4)
            def _(i):
                both = rim[side, i]
                swapped = jnp.concatenate([both[:, 64:], both[:, :64]], axis=1)
                early, late = (both, swapped) if side == 0 else (swapped, both)
                for k, own in ((0, early), (HR // 2, late)):
                    pooled[first + i + k, :, 128:] = jnp.where(keep, own, zero)

            start = HR - SPR if side == 0 else rows + HR

            @pl.loop(0, SPR // 2, unroll=2)
            def _(i):
                both = rim_side[side, i]
                swapped = jnp.concatenate([both[:, 64:], both[:, :64]], axis=1)
                early, late = (swapped, both) if side == 0 else (both, swapped)
                for k, own in ((0, early), (SPR // 2, late)):
                    pooled[start + i + k, :, :128] = jnp.where(keep, zero, own)

    run_pair(0, rows - SPR, SPR, 256, 256)

    edge_out[0, :, :64] = sums[192:, :64]
    edge_out[0, :, 64:] = sums[192:, 192:]
    edge_out[1, :, :64] = sums[128:192, 128:192]
    edge_out[1, :, 64:] = sums[128:192, 64:128]
    edges = both_ways(edge_out, edge_in, edge_send, edge_recv)
    send(edges)

    total = HR + GROUP - SPR
    run_pair(SPR, rows - HR - GROUP, total, 128, 256)

    table_copy.wait()
    for r in range(2, rounds):
        pass_on(r)
    pl.semaphore_wait(vouch.at[rounds - 1], 1)
    for side in range(2):
        @pl.when(receives[side])
        def _():
            edges[side].wait_recv()

        @pl.when(~receives[side])
        def _():
            edge_in[side] = jnp.zeros((nodes, 128), F32)

    early, late = edge_in[0], edge_in[1]
    front0 = jnp.concatenate([sums[64:128, 128:192], sums[64:128, 64:128]], axis=1) + early
    front1 = jnp.concatenate([sums[:64, 64:128], sums[:64, :64] + late[:, :64]], axis=1)
    tails = jnp.concatenate([sums[64:128, :64], sums[:64, 192:] + late[:, 64:]], axis=1)
    lines = nodes // TEAM
    for s in range(TEAM):
        part = slice(s * lines, (s + 1) * lines)
        piece_out[s, : 2 * lines] = jnp.concatenate([front0[part], front1[part]], axis=0).astype(BF16)
        piece_out[s, 2 * lines :] = tails[part].astype(BF16)

    def piece_copy(d):
        there = lax.rem(me + d, count)
        return pltpu.make_async_remote_copy(
            src_ref=piece_out.at[lax.rem(there, TEAM)],
            dst_ref=spread.at[me],
            send_sem=piece_send,
            recv_sem=piece_recv,
            device_id=place_of(there),
            device_id_type=MESH,
        )

    @pl.loop(1, count)
    def _(d):
        piece_copy(d).start()

    spread[me] = piece_out[seat]

    others = spread.at[pl.ds(0, count - 1)]
    all_pieces = pltpu.make_async_remote_copy(
        src_ref=others, dst_ref=others, send_sem=piece_send, recv_sem=piece_recv,
        device_id=after, device_id_type=MESH,
    )
    all_pieces.wait_recv()

    low = lax.broadcasted_iota(jnp.int32, (lines, 128), 1) < 64

    def fill(there, box):
        fronts, ends_of = [], []
        for s in range(OWNMAX):
            entry = table[0, there * OWNMAX + s]
            agg = jnp.maximum(entry - 1, 0)
            which = lax.rem(agg, LW)
            piece = spread[agg // LW].astype(F32)
            front = jnp.where(which == 1, piece[lines : 2 * lines], piece[:lines])
            fronts.append(jnp.where(entry > 0, front, 0.0))
            tail = piece[2 * lines :]
            swapped = jnp.concatenate([tail[:, 64:], tail[:, :64]], axis=1)
            tail = jnp.where(which == s % 2, tail, swapped)
            ends_of.append(jnp.where(entry > 0, tail, 0.0))
        for k in range(OWNMAX // 2):
            box[k] = jnp.concatenate(fronts[2 * k : 2 * k + 2], axis=0).astype(BF16)
        tails = [jnp.where(low, ends_of[2 * k], ends_of[2 * k + 1]) for k in range(OWNMAX // 2)]
        for k in range(OWNMAX // 4):
            box[OWNMAX // 2 + k] = jnp.concatenate(tails[2 * k : 2 * k + 2], axis=0).astype(BF16)

    def mail_copy(d):
        return pltpu.make_async_remote_copy(
            src_ref=mail_out.at[d],
            dst_ref=mail_in.at[seat],
            send_sem=mail_send,
            recv_sem=mail_recv,
            device_id=place_of(mate(d)),
            device_id_type=MESH,
        )

    @pl.loop(1, TEAM, unroll=7)
    def _(d):
        fill(lax.rem(seat + d, TEAM), mail_out.at[d])
        mail_copy(d).start()

    fill(seat, mail_in.at[seat])

    boxes = mail_in.at[pl.ds(0, TEAM - 1)]
    all_mail = pltpu.make_async_remote_copy(
        src_ref=boxes, dst_ref=boxes, send_sem=mail_send, recv_sem=mail_recv,
        device_id=after, device_id_type=MESH,
    )
    all_mail.wait_recv()

    for m in range(TEAM // 2):
        span = pl.ds(2 * lines * m, 2 * lines)
        for k in range(OWNMAX // 2):
            one, two = (mail_in[2 * m + q, k].astype(F32) for q in range(2))
            for h in range(2):
                part = slice(h * lines, (h + 1) * lines)
                out[2 * k + h, span, :128] = jnp.concatenate([one[part], two[part]], axis=0).astype(BF16)
        for k in range(OWNMAX // 4):
            one, two = (mail_in[2 * m + q, OWNMAX // 2 + k].astype(F32) for q in range(2))
            for h in range(2):
                part = slice(h * lines, (h + 1) * lines)
                both = jnp.concatenate([one[part], two[part]], axis=0).astype(BF16)
                out[4 * k + 2 * h, span, 128:] = both[:, :64]
                out[4 * k + 2 * h + 1, span, 128:] = both[:, 64:]

    for side in range(2):
        @pl.when(sends[side])
        def _():
            rims[side].wait_send()
            spills[side].wait_send()
            edges[side].wait_send()

    all_pieces.wait_send()

    all_mail.wait_send()


def shards(a_blocks, a_columns, p_blocks, p_pattern, aggregate, owner_map):
    rows, nodes = a_blocks.shape[:2]
    count = lax.axis_size(AXES)
    vmem = pl.BlockSpec(memory_space=pltpu.VMEM)
    hbm = pl.BlockSpec(memory_space=pl.ANY)
    lines = nodes // TEAM
    half = OWNMAX // 2 + OWNMAX // 4
    dma = pltpu.SemaphoreType.DMA
    pool = (rows + 2 * HR, nodes, 4 * nodes)
    total_agg = owner_map.shape[0]
    return pl.pallas_call(
        kernel,
        out_shape=jax.ShapeDtypeStruct((OWNMAX, nodes, 3 * nodes), BF16),
        in_specs=[hbm] * 6,
        out_specs=vmem,
        scratch_shapes=[
            pltpu.SMEM((a_columns.shape[1], rows), jnp.int32),
            pltpu.SMEM((3, rows), jnp.int32),
            pltpu.SMEM((1, rows), jnp.int32),
            pltpu.VMEM((1, total_agg), jnp.int32),
            pltpu.VMEM(a_blocks.shape, BF16),
            pltpu.VMEM(p_blocks.shape, BF16),
            pltpu.VMEM(pool, BF16),
            pltpu.VMEM((2, (HR + GROUP - SPR) * nodes, 4 * nodes), BF16),
            pltpu.VMEM((4 * nodes, 4 * nodes), F32),
            pltpu.VMEM((2, HR // 2, nodes, 2 * nodes), BF16),
            pltpu.VMEM((2, SPR // 2, nodes, 2 * nodes), BF16),
            pltpu.VMEM((2, HR // 2, nodes, 2 * nodes), BF16),
            pltpu.VMEM((2, SPR // 2, nodes, 2 * nodes), BF16),
            pltpu.VMEM((2, nodes, 2 * nodes), F32),
            pltpu.VMEM((2, nodes, 2 * nodes), F32),
            pltpu.VMEM((TEAM, 3 * lines, 128), BF16),
            pltpu.VMEM((count, 3 * lines, 128), BF16),
            pltpu.VMEM((TEAM, half, 2 * lines, 128), BF16),
            pltpu.VMEM((TEAM, half, 2 * lines, 128), BF16),
            pltpu.VMEM((8, 128), jnp.int32),
            pltpu.SMEM((8, 128), jnp.int32),
            dma((rows // 4 // GROUP + 2,)),
            dma((4,)),
            dma((5,)),
            dma((2,)),
            dma((2,)),
            dma((2,)),
            dma((2,)),
            dma((2,)),
            dma((2,)),
            dma,
            dma,
            dma,
            dma,
            pltpu.SemaphoreType.REGULAR((count.bit_length() - TEAM.bit_length(),)),
        ],
        compiler_params=pltpu.CompilerParams(
            collective_id=0, has_side_effects=True, vmem_limit_bytes=56 << 20
        ),
    )(a_blocks, a_columns.T, p_blocks, p_pattern.T, aggregate[None], owner_map[None])


def solution(mesh):
    placed = (
        P(AXES, None, None),
        P(AXES, None),
        P(AXES, None, None),
        P(AXES, None),
        P(AXES),
        P(),
    )
    return jax.shard_map(
        shards,
        mesh=mesh,
        in_specs=placed,
        out_specs=P(AXES, None, None),
        check_vma=False,
    )
```

```python
import jax
import jax.numpy as jnp
from jax import lax
from jax.experimental import pallas as pl
from jax.experimental.pallas import tpu as pltpu
from jax.sharding import PartitionSpec as P

HR = 32
LW = 2
OWNMAX = 8
GROUP = 16
SPR = 8
TEAM = 8
AXES = ("wide", "narrow")
MESH = pl.DeviceIdType.MESH
BF16 = jnp.bfloat16
F32 = jnp.float32


def kernel(a_hbm, cols_hbm, p_hbm, pattern_hbm, aggregate_hbm, owners_hbm, out,
           cols, pattern, aggregate, owners, a_v, p_v, pooled, applied, sums, packed, packed_side, rim, rim_side,
           edge_out, edge_in, piece_out, spread, mail_out, mail_in, table_v, table,
           a_sem, p_sem, index_sem, rim_send, rim_recv, spill_send, spill_recv, edge_send, edge_recv,
           piece_send, piece_recv, mail_send, mail_recv, vouch):
    rows, nodes = a_hbm.shape[0], a_hbm.shape[1]
    me = lax.axis_index(AXES)
    narrow = lax.axis_size("narrow")
    count = lax.axis_size(AXES)
    teams = count // TEAM
    rounds = teams.bit_length() - 1
    team, seat = me // TEAM, lax.rem(me, TEAM)
    groups = rows // GROUP
    has_before, has_after = me > 0, me < count - 1

    def place_of(device):
        return (device // narrow, lax.rem(device, narrow))

    def mate(d):
        return team * TEAM + lax.rem(seat + d, TEAM)

    def partner(r):
        step = TEAM << r
        up = lax.rem(me // step, 2) == 0
        return place_of(jnp.where(up, me + step, me - step))

    after = place_of(jnp.minimum(me + 1, count - 1))
    before = place_of(jnp.maximum(me - 1, 0))
    barrier = pltpu.get_barrier_semaphore()

    @pl.when(has_after)
    def _():
        pl.semaphore_signal(barrier, inc=1, device_id=after, device_id_type=MESH)

    @pl.when(has_before)
    def _():
        pl.semaphore_signal(barrier, inc=1, device_id=before, device_id_type=MESH)

    @pl.loop(1, TEAM)
    def _(d):
        pl.semaphore_signal(barrier, inc=1, device_id=place_of(mate(d)), device_id_type=MESH)

    for r in range(rounds):
        pl.semaphore_signal(barrier, inc=1, device_id=partner(r), device_id_type=MESH)

    step = 2 * GROUP

    def p_copy(k):
        first = (0, rows - step, step, rows // 2)[k]
        span = pl.ds(first, step if k < 2 else rows // 2 - step)
        return pltpu.make_async_copy(p_hbm.at[span], p_v.at[span], p_sem.at[k])

    wing = rows // 4
    inner = (rows - 2 * wing) // step

    def a_copy(first, total, k):
        span = pl.ds(first, total)
        return pltpu.make_async_copy(a_hbm.at[span], a_v.at[span], a_sem.at[k])

    def a_inner(k):
        return a_copy(wing + k * step, step, k)

    a_wings = [a_copy(first, wing, inner + k) for k, first in enumerate((0, rows - wing))]

    for k in range(2):
        p_copy(k).start()
    index_copies = [
        pltpu.make_async_copy(source, landing, index_sem.at[k])
        for k, (source, landing) in enumerate(
            (
                (pattern_hbm, pattern),
                (aggregate_hbm, aggregate),
                (owners_hbm, owners),
                (cols_hbm, cols),
            )
        )
    ]
    for copy in index_copies:
        copy.start()

    left = lax.broadcasted_iota(jnp.int32, (nodes, 128), 1) < 64
    lane = lax.broadcasted_iota(jnp.int32, (1, 128), 1) < 64

    def place_group(g, at_end):
        for j in range(GROUP):
            i = g * GROUP + j
            second = jnp.where(aggregate[0, i] - me * LW == 1, 1.0, 0.0)
            has0 = pattern[0, i].astype(F32)
            has2 = pattern[2, i].astype(F32)
            x0 = p_v[i, :, :128]
            x2 = p_v[i, :, 128:]
            swapped = jnp.concatenate([x0[:, 64:], x0[:, :64]], axis=1)
            mixed = jnp.concatenate([x2, x0[:, 64:]], axis=1)
            one = jnp.where(lane, second, second * has0).astype(BF16)
            two = jnp.where(lane, (1.0 - second) * has2, 1.0 - second).astype(BF16)
            pooled[HR + i, :, :128] = swapped * one + mixed * two
            if at_end:
                three = jnp.where(lane, (1.0 - second) * has0, second * has2).astype(BF16)
                pooled[HR + i, :, 128:] = jnp.concatenate([x0[:, :64], x2], axis=1) * three
            else:
                pooled[HR + i, :, 128:] = jnp.zeros_like(x0)

    for k in range(2):
        p_copy(k).wait()
    for k in range(2, 4):
        p_copy(k).start()
    for k in range(inner):
        a_inner(k).start()
    for copy in a_wings:
        copy.start()

    @pl.loop(0, HR // 2, unroll=4)
    def _(i):
        for side, first in ((0, rows - HR), (1, 0)):
            packed[side, i] = jnp.concatenate(
                [p_v[first + i + k, :, 64:128] for k in (0, HR // 2)], axis=1
            )

    near = TEAM - 1 + rounds + jnp.where(has_after, 1, 0) + jnp.where(has_before, 1, 0)
    pl.semaphore_wait(barrier, near)

    def both_ways(outbox, inbox, send_sem, recv_sem):
        return [
            pltpu.make_async_remote_copy(
                src_ref=outbox.at[side],
                dst_ref=inbox.at[side],
                send_sem=send_sem.at[side],
                recv_sem=recv_sem.at[side],
                device_id=(after, before)[side],
                device_id_type=MESH,
            )
            for side in range(2)
        ]

    sends = (has_after, has_before)
    receives = (has_before, has_after)
    def send(copies):
        for side in range(2):
            @pl.when(sends[side])
            def _():
                copies[side].start()

    rims = both_ways(packed, rim, rim_send, rim_recv)
    spills = both_ways(packed_side, rim_side, spill_send, spill_recv)
    send(rims)

    def vouch_for(r):
        pl.semaphore_signal(vouch.at[r], inc=1, device_id=partner(r), device_id_type=MESH)

    def pass_on(r):
        pl.semaphore_wait(vouch.at[r - 1], 1)
        vouch_for(r)

    vouch_for(0)
    for copy in index_copies:
        copy.wait()

    @pl.loop(0, 2)
    def _(end):
        place_group(end * (groups - 1), True)

    @pl.loop(0, SPR // 2, unroll=2)
    def _(i):
        for side, first, at in ((0, HR + rows - SPR, 192), (1, HR, 128)):
            packed_side[side, i] = jnp.concatenate(
                [pooled[first + i + k, :, at : at + 64] for k in (0, SPR // 2)], axis=1
            )

    send(spills)

    total_agg = owners.shape[1]
    down = lax.broadcasted_iota(jnp.int32, (total_agg, total_agg), 0)
    over = lax.broadcasted_iota(jnp.int32, (total_agg, total_agg), 1)
    owner_row = owners[...]
    owner_col = jnp.sum(jnp.where(down == over, owner_row, 0), axis=1, keepdims=True)
    rank = jnp.sum(jnp.where((owner_col == owner_row) & (over < down), 1, 0), axis=1, keepdims=True)
    wanted = lax.broadcasted_iota(jnp.int32, (total_agg, 128), 1) + team * (TEAM * OWNMAX)
    number = lax.broadcasted_iota(jnp.int32, (total_agg, 128), 0) + 1
    hit = (owner_col * OWNMAX + rank) == wanted
    found = jnp.sum(jnp.where(hit, number, 0), axis=0, keepdims=True)
    table_v[...] = jnp.broadcast_to(found, table_v.shape)
    table_copy = pltpu.make_async_copy(table_v, table, index_sem.at[4])
    table_copy.start()

    @pl.loop(0, 2)
    def _(end):
        place_group(1 + end * (groups - 3), False)

    @pl.loop(0, HR)
    def _(i):
        pooled[i] = jnp.zeros((nodes, 256), BF16)
        pooled[rows + HR + i] = jnp.zeros((nodes, 256), BF16)

    sums[...] = jnp.zeros_like(sums)
    for k in range(2, 4):
        p_copy(k).wait()

    @pl.loop(2, groups - 2, unroll=2)
    def _(g):
        place_group(g, False)

    base = HR - me * rows

    def apply_rows(first, total, buffer, width):
        for j in range(total):
            i = first + j
            stack = jnp.concatenate(
                [pooled[jnp.maximum(cols[k, i] + base, 0), :, :width] for k in range(8)], axis=0
            )
            product = jnp.dot(a_v[i], stack, preferred_element_type=F32)
            applied[buffer, j * nodes : (j + 1) * nodes, :width] = product.astype(BF16)

    def add_up(first, total, buffer, high, width):
        left_rows = pooled[pl.ds(HR + first, total), :, :high].reshape(total * nodes, high)
        sums[:high, :width] += lax.dot_general(
            left_rows, applied[buffer, : total * nodes, :width], (((0,), (0,)), ((), ())),
            preferred_element_type=F32,
        )

    def run_pair(first, later, total, high, width):
        apply_rows(first, total, 0, width)
        apply_rows(later, total, 1, width)
        add_up(first, total, 0, high, width)
        add_up(later, total, 1, high, width)

    @pl.loop(0, inner, unroll=inner)
    def _(k):
        a_inner(k).wait()
        first = wing + k * step
        run_pair(first, first + GROUP, GROUP, 128, 128)

    for copy in a_wings:
        copy.wait()
    pass_on(1)

    zero = jnp.zeros((nodes, 128), BF16)
    for side, first in enumerate((0, rows + HR)):
        @pl.when(receives[side])
        def _():
            rims[side].wait_recv()
            spills[side].wait_recv()
            keep = left if side == 0 else ~left

            @pl.loop(0, HR // 2, unroll=4)
            def _(i):
                both = rim[side, i]
                swapped = jnp.concatenate([both[:, 64:], both[:, :64]], axis=1)
                early, late = (both, swapped) if side == 0 else (swapped, both)
                for k, own in ((0, early), (HR // 2, late)):
                    pooled[first + i + k, :, 128:] = jnp.where(keep, own, zero)

            start = HR - SPR if side == 0 else rows + HR

            @pl.loop(0, SPR // 2, unroll=2)
            def _(i):
                both = rim_side[side, i]
                swapped = jnp.concatenate([both[:, 64:], both[:, :64]], axis=1)
                early, late = (swapped, both) if side == 0 else (both, swapped)
                for k, own in ((0, early), (SPR // 2, late)):
                    pooled[start + i + k, :, :128] = jnp.where(keep, zero, own)

    run_pair(0, rows - SPR, SPR, 256, 256)

    edge_out[0, :, :64] = sums[192:, :64]
    edge_out[0, :, 64:] = sums[192:, 192:]
    edge_out[1, :, :64] = sums[128:192, 128:192]
    edge_out[1, :, 64:] = sums[128:192, 64:128]
    edges = both_ways(edge_out, edge_in, edge_send, edge_recv)
    send(edges)

    total = HR + GROUP - SPR
    run_pair(SPR, rows - HR - GROUP, total, 128, 256)

    table_copy.wait()
    for r in range(2, rounds):
        pass_on(r)
    pl.semaphore_wait(vouch.at[rounds - 1], 1)
    for side in range(2):
        @pl.when(receives[side])
        def _():
            edges[side].wait_recv()

        @pl.when(~receives[side])
        def _():
            edge_in[side] = jnp.zeros((nodes, 128), F32)

    early, late = edge_in[0], edge_in[1]
    front0 = jnp.concatenate([sums[64:128, 128:192], sums[64:128, 64:128]], axis=1) + early
    front1 = jnp.concatenate([sums[:64, 64:128], sums[:64, :64] + late[:, :64]], axis=1)
    tails = jnp.concatenate([sums[64:128, :64], sums[:64, 192:] + late[:, 64:]], axis=1)
    lines = nodes // TEAM
    for s in range(TEAM):
        part = slice(s * lines, (s + 1) * lines)
        piece_out[s, : 2 * lines] = jnp.concatenate([front0[part], front1[part]], axis=0).astype(BF16)
        piece_out[s, 2 * lines :] = tails[part].astype(BF16)

    def piece_copy(d):
        there = lax.rem(me + d, count)
        return pltpu.make_async_remote_copy(
            src_ref=piece_out.at[lax.rem(there, TEAM)],
            dst_ref=spread.at[me],
            send_sem=piece_send,
            recv_sem=piece_recv,
            device_id=place_of(there),
            device_id_type=MESH,
        )

    @pl.loop(1, count)
    def _(d):
        piece_copy(d).start()

    spread[me] = piece_out[seat]

    others = spread.at[pl.ds(0, count - 1)]
    all_pieces = pltpu.make_async_remote_copy(
        src_ref=others, dst_ref=others, send_sem=piece_send, recv_sem=piece_recv,
        device_id=after, device_id_type=MESH,
    )
    all_pieces.wait_recv()

    low = lax.broadcasted_iota(jnp.int32, (lines, 128), 1) < 64

    def fill(there, box):
        fronts, ends_of = [], []
        for s in range(OWNMAX):
            entry = table[0, there * OWNMAX + s]
            agg = jnp.maximum(entry - 1, 0)
            which = lax.rem(agg, LW)
            piece = spread[agg // LW].astype(F32)
            front = jnp.where(which == 1, piece[lines : 2 * lines], piece[:lines])
            fronts.append(jnp.where(entry > 0, front, 0.0))
            tail = piece[2 * lines :]
            swapped = jnp.concatenate([tail[:, 64:], tail[:, :64]], axis=1)
            tail = jnp.where(which == s % 2, tail, swapped)
            ends_of.append(jnp.where(entry > 0, tail, 0.0))
        for k in range(OWNMAX // 2):
            box[k] = jnp.concatenate(fronts[2 * k : 2 * k + 2], axis=0).astype(BF16)
        tails = [jnp.where(low, ends_of[2 * k], ends_of[2 * k + 1]) for k in range(OWNMAX // 2)]
        for k in range(OWNMAX // 4):
            box[OWNMAX // 2 + k] = jnp.concatenate(tails[2 * k : 2 * k + 2], axis=0).astype(BF16)

    def mail_copy(d):
        return pltpu.make_async_remote_copy(
            src_ref=mail_out.at[d],
            dst_ref=mail_in.at[seat],
            send_sem=mail_send,
            recv_sem=mail_recv,
            device_id=place_of(mate(d)),
            device_id_type=MESH,
        )

    @pl.loop(1, TEAM, unroll=7)
    def _(d):
        fill(lax.rem(seat + d, TEAM), mail_out.at[d])
        mail_copy(d).start()

    fill(seat, mail_in.at[seat])

    boxes = mail_in.at[pl.ds(0, TEAM - 1)]
    all_mail = pltpu.make_async_remote_copy(
        src_ref=boxes, dst_ref=boxes, send_sem=mail_send, recv_sem=mail_recv,
        device_id=after, device_id_type=MESH,
    )
    all_mail.wait_recv()

    for m in range(TEAM // 2):
        span = pl.ds(2 * lines * m, 2 * lines)
        for k in range(OWNMAX // 2):
            one, two = (mail_in[2 * m + q, k].astype(F32) for q in range(2))
            for h in range(2):
                part = slice(h * lines, (h + 1) * lines)
                out[2 * k + h, span, :128] = jnp.concatenate([one[part], two[part]], axis=0).astype(BF16)
        for k in range(OWNMAX // 4):
            one, two = (mail_in[2 * m + q, OWNMAX // 2 + k].astype(F32) for q in range(2))
            for h in range(2):
                part = slice(h * lines, (h + 1) * lines)
                both = jnp.concatenate([one[part], two[part]], axis=0).astype(BF16)
                out[4 * k + 2 * h, span, 128:] = both[:, :64]
                out[4 * k + 2 * h + 1, span, 128:] = both[:, 64:]

    for side in range(2):
        @pl.when(sends[side])
        def _():
            rims[side].wait_send()
            spills[side].wait_send()
            edges[side].wait_send()

    all_pieces.wait_send()

    all_mail.wait_send()


def shards(a_blocks, a_columns, p_blocks, p_pattern, aggregate, owner_map):
    rows, nodes = a_blocks.shape[:2]
    count = lax.axis_size(AXES)
    vmem = pl.BlockSpec(memory_space=pltpu.VMEM)
    hbm = pl.BlockSpec(memory_space=pl.ANY)
    lines = nodes // TEAM
    half = OWNMAX // 2 + OWNMAX // 4
    dma = pltpu.SemaphoreType.DMA
    pool = (rows + 2 * HR, nodes, 4 * nodes)
    total_agg = owner_map.shape[0]
    return pl.pallas_call(
        kernel,
        out_shape=jax.ShapeDtypeStruct((OWNMAX, nodes, 3 * nodes), BF16),
        in_specs=[hbm] * 6,
        out_specs=vmem,
        scratch_shapes=[
            pltpu.SMEM((a_columns.shape[1], rows), jnp.int32),
            pltpu.SMEM((3, rows), jnp.int32),
            pltpu.SMEM((1, rows), jnp.int32),
            pltpu.VMEM((1, total_agg), jnp.int32),
            pltpu.VMEM(a_blocks.shape, BF16),
            pltpu.VMEM(p_blocks.shape, BF16),
            pltpu.VMEM(pool, BF16),
            pltpu.VMEM((2, (HR + GROUP - SPR) * nodes, 4 * nodes), BF16),
            pltpu.VMEM((4 * nodes, 4 * nodes), F32),
            pltpu.VMEM((2, HR // 2, nodes, 2 * nodes), BF16),
            pltpu.VMEM((2, SPR // 2, nodes, 2 * nodes), BF16),
            pltpu.VMEM((2, HR // 2, nodes, 2 * nodes), BF16),
            pltpu.VMEM((2, SPR // 2, nodes, 2 * nodes), BF16),
            pltpu.VMEM((2, nodes, 2 * nodes), F32),
            pltpu.VMEM((2, nodes, 2 * nodes), F32),
            pltpu.VMEM((TEAM, 3 * lines, 128), BF16),
            pltpu.VMEM((count, 3 * lines, 128), BF16),
            pltpu.VMEM((TEAM, half, 2 * lines, 128), BF16),
            pltpu.VMEM((TEAM, half, 2 * lines, 128), BF16),
            pltpu.VMEM((8, 128), jnp.int32),
            pltpu.SMEM((8, 128), jnp.int32),
            dma((rows // 4 // GROUP + 2,)),
            dma((4,)),
            dma((5,)),
            dma((2,)),
            dma((2,)),
            dma((2,)),
            dma((2,)),
            dma((2,)),
            dma((2,)),
            dma,
            dma,
            dma,
            dma,
            pltpu.SemaphoreType.REGULAR((count.bit_length() - TEAM.bit_length(),)),
        ],
        compiler_params=pltpu.CompilerParams(
            collective_id=0, has_side_effects=True, vmem_limit_bytes=56 << 20
        ),
    )(a_blocks, a_columns.T, p_blocks, p_pattern.T, aggregate[None], owner_map[None])


def solution(mesh):
    placed = (
        P(AXES, None, None),
        P(AXES, None),
        P(AXES, None, None),
        P(AXES, None),
        P(AXES),
        P(),
    )
    return jax.shard_map(
        shards,
        mesh=mesh,
        in_specs=placed,
        out_specs=P(AXES, None, None),
        check_vma=False,
    )
```

```python
import jax
import jax.numpy as jnp
from jax import lax
from jax.experimental import pallas as pl
from jax.experimental.pallas import tpu as pltpu
from jax.sharding import PartitionSpec as P

HR = 32
LW = 2
OWNMAX = 8
GROUP = 16
SPR = 8
TEAM = 8
AXES = ("wide", "narrow")
MESH = pl.DeviceIdType.MESH
BF16 = jnp.bfloat16
F32 = jnp.float32


def kernel(a_hbm, cols_hbm, p_hbm, pattern_hbm, aggregate_hbm, owners_hbm, out,
           cols, pattern, aggregate, owners, a_v, p_v, pooled, applied, sums, packed, packed_side, rim, rim_side,
           edge_out, edge_in, piece_out, spread, mail_out, mail_in, table_v, table,
           a_sem, p_sem, index_sem, rim_send, rim_recv, spill_send, spill_recv, edge_send, edge_recv,
           piece_send, piece_recv, mail_send, mail_recv, vouch):
    rows, nodes = a_hbm.shape[0], a_hbm.shape[1]
    me = lax.axis_index(AXES)
    narrow = lax.axis_size("narrow")
    count = lax.axis_size(AXES)
    teams = count // TEAM
    rounds = teams.bit_length() - 1
    team, seat = me // TEAM, lax.rem(me, TEAM)
    groups = rows // GROUP
    has_before, has_after = me > 0, me < count - 1

    def place_of(device):
        return (device // narrow, lax.rem(device, narrow))

    def mate(d):
        return team * TEAM + lax.rem(seat + d, TEAM)

    def partner(r):
        step = TEAM << r
        up = lax.rem(me // step, 2) == 0
        return place_of(jnp.where(up, me + step, me - step))

    after = place_of(jnp.minimum(me + 1, count - 1))
    before = place_of(jnp.maximum(me - 1, 0))
    barrier = pltpu.get_barrier_semaphore()

    @pl.when(has_after)
    def _():
        pl.semaphore_signal(barrier, inc=1, device_id=after, device_id_type=MESH)

    @pl.when(has_before)
    def _():
        pl.semaphore_signal(barrier, inc=1, device_id=before, device_id_type=MESH)

    @pl.loop(1, TEAM)
    def _(d):
        pl.semaphore_signal(barrier, inc=1, device_id=place_of(mate(d)), device_id_type=MESH)

    for r in range(rounds):
        pl.semaphore_signal(barrier, inc=1, device_id=partner(r), device_id_type=MESH)

    step = 2 * GROUP

    def p_copy(k):
        first = (0, rows - step, step, rows // 2)[k]
        span = pl.ds(first, step if k < 2 else rows // 2 - step)
        return pltpu.make_async_copy(p_hbm.at[span], p_v.at[span], p_sem.at[k])

    wing = rows // 4
    inner = (rows - 2 * wing) // step

    def a_copy(first, total, k):
        span = pl.ds(first, total)
        return pltpu.make_async_copy(a_hbm.at[span], a_v.at[span], a_sem.at[k])

    def a_inner(k):
        return a_copy(wing + k * step, step, k)

    a_wings = [a_copy(first, wing, inner + k) for k, first in enumerate((0, rows - wing))]

    for k in range(2):
        p_copy(k).start()
    index_copies = [
        pltpu.make_async_copy(source, landing, index_sem.at[k])
        for k, (source, landing) in enumerate(
            (
                (pattern_hbm, pattern),
                (aggregate_hbm, aggregate),
                (owners_hbm, owners),
                (cols_hbm, cols),
            )
        )
    ]
    for copy in index_copies:
        copy.start()

    left = lax.broadcasted_iota(jnp.int32, (nodes, 128), 1) < 64
    lane = lax.broadcasted_iota(jnp.int32, (1, 128), 1) < 64

    def place_group(g, at_end):
        for j in range(GROUP):
            i = g * GROUP + j
            second = jnp.where(aggregate[0, i] - me * LW == 1, 1.0, 0.0)
            has0 = pattern[0, i].astype(F32)
            has2 = pattern[2, i].astype(F32)
            x0 = p_v[i, :, :128]
            x2 = p_v[i, :, 128:]
            swapped = jnp.concatenate([x0[:, 64:], x0[:, :64]], axis=1)
            mixed = jnp.concatenate([x2, x0[:, 64:]], axis=1)
            one = jnp.where(lane, second, second * has0).astype(BF16)
            two = jnp.where(lane, (1.0 - second) * has2, 1.0 - second).astype(BF16)
            pooled[HR + i, :, :128] = swapped * one + mixed * two
            if at_end:
                three = jnp.where(lane, (1.0 - second) * has0, second * has2).astype(BF16)
                pooled[HR + i, :, 128:] = jnp.concatenate([x0[:, :64], x2], axis=1) * three
            else:
                pooled[HR + i, :, 128:] = jnp.zeros_like(x0)

    for k in range(2):
        p_copy(k).wait()
    for k in range(2, 4):
        p_copy(k).start()
    for k in range(inner):
        a_inner(k).start()
    for copy in a_wings:
        copy.start()

    @pl.loop(0, HR // 2, unroll=4)
    def _(i):
        for side, first in ((0, rows - HR), (1, 0)):
            packed[side, i] = jnp.concatenate(
                [p_v[first + i + k, :, 64:128] for k in (0, HR // 2)], axis=1
            )

    near = TEAM - 1 + rounds + jnp.where(has_after, 1, 0) + jnp.where(has_before, 1, 0)
    pl.semaphore_wait(barrier, near)

    def both_ways(outbox, inbox, send_sem, recv_sem):
        return [
            pltpu.make_async_remote_copy(
                src_ref=outbox.at[side],
                dst_ref=inbox.at[side],
                send_sem=send_sem.at[side],
                recv_sem=recv_sem.at[side],
                device_id=(after, before)[side],
                device_id_type=MESH,
            )
            for side in range(2)
        ]

    sends = (has_after, has_before)
    receives = (has_before, has_after)
    def send(copies):
        for side in range(2):
            @pl.when(sends[side])
            def _():
                copies[side].start()

    rims = both_ways(packed, rim, rim_send, rim_recv)
    spills = both_ways(packed_side, rim_side, spill_send, spill_recv)
    send(rims)

    def vouch_for(r):
        pl.semaphore_signal(vouch.at[r], inc=1, device_id=partner(r), device_id_type=MESH)

    def pass_on(r):
        pl.semaphore_wait(vouch.at[r - 1], 1)
        vouch_for(r)

    vouch_for(0)
    for copy in index_copies:
        copy.wait()

    @pl.loop(0, 2)
    def _(end):
        place_group(end * (groups - 1), True)

    @pl.loop(0, SPR // 2, unroll=2)
    def _(i):
        for side, first, at in ((0, HR + rows - SPR, 192), (1, HR, 128)):
            packed_side[side, i] = jnp.concatenate(
                [pooled[first + i + k, :, at : at + 64] for k in (0, SPR // 2)], axis=1
            )

    send(spills)

    total_agg = owners.shape[1]
    down = lax.broadcasted_iota(jnp.int32, (total_agg, total_agg), 0)
    over = lax.broadcasted_iota(jnp.int32, (total_agg, total_agg), 1)
    owner_row = owners[...]
    owner_col = jnp.sum(jnp.where(down == over, owner_row, 0), axis=1, keepdims=True)
    rank = jnp.sum(jnp.where((owner_col == owner_row) & (over < down), 1, 0), axis=1, keepdims=True)
    wanted = lax.broadcasted_iota(jnp.int32, (total_agg, 128), 1) + team * (TEAM * OWNMAX)
    number = lax.broadcasted_iota(jnp.int32, (total_agg, 128), 0) + 1
    hit = (owner_col * OWNMAX + rank) == wanted
    found = jnp.sum(jnp.where(hit, number, 0), axis=0, keepdims=True)
    table_v[...] = jnp.broadcast_to(found, table_v.shape)
    table_copy = pltpu.make_async_copy(table_v, table, index_sem.at[4])
    table_copy.start()

    @pl.loop(0, 2)
    def _(end):
        place_group(1 + end * (groups - 3), False)

    @pl.loop(0, HR, unroll=4)
    def _(i):
        pooled[i] = jnp.zeros((nodes, 256), BF16)
        pooled[rows + HR + i] = jnp.zeros((nodes, 256), BF16)

    sums[...] = jnp.zeros_like(sums)
    for k in range(2, 4):
        p_copy(k).wait()

    @pl.loop(2, groups - 2, unroll=2)
    def _(g):
        place_group(g, False)

    base = HR - me * rows

    def apply_rows(first, total, buffer, width):
        for j in range(total):
            i = first + j
            stack = jnp.concatenate(
                [pooled[jnp.maximum(cols[k, i] + base, 0), :, :width] for k in range(8)], axis=0
            )
            product = jnp.dot(a_v[i], stack, preferred_element_type=F32)
            applied[buffer, j * nodes : (j + 1) * nodes, :width] = product.astype(BF16)

    def add_up(first, total, buffer, high, width):
        left_rows = pooled[pl.ds(HR + first, total), :, :high].reshape(total * nodes, high)
        sums[:high, :width] += lax.dot_general(
            left_rows, applied[buffer, : total * nodes, :width], (((0,), (0,)), ((), ())),
            preferred_element_type=F32,
        )

    def run_pair(first, later, total, high, width):
        apply_rows(first, total, 0, width)
        apply_rows(later, total, 1, width)
        add_up(first, total, 0, high, width)
        add_up(later, total, 1, high, width)

    @pl.loop(0, inner, unroll=inner)
    def _(k):
        a_inner(k).wait()
        first = wing + k * step
        run_pair(first, first + GROUP, GROUP, 128, 128)

    for copy in a_wings:
        copy.wait()
    pass_on(1)

    zero = jnp.zeros((nodes, 128), BF16)
    for side, first in enumerate((0, rows + HR)):
        @pl.when(receives[side])
        def _():
            rims[side].wait_recv()
            spills[side].wait_recv()
            keep = left if side == 0 else ~left

            @pl.loop(0, HR // 2, unroll=4)
            def _(i):
                both = rim[side, i]
                swapped = jnp.concatenate([both[:, 64:], both[:, :64]], axis=1)
                early, late = (both, swapped) if side == 0 else (swapped, both)
                for k, own in ((0, early), (HR // 2, late)):
                    pooled[first + i + k, :, 128:] = jnp.where(keep, own, zero)

            start = HR - SPR if side == 0 else rows + HR

            @pl.loop(0, SPR // 2, unroll=2)
            def _(i):
                both = rim_side[side, i]
                swapped = jnp.concatenate([both[:, 64:], both[:, :64]], axis=1)
                early, late = (swapped, both) if side == 0 else (both, swapped)
                for k, own in ((0, early), (SPR // 2, late)):
                    pooled[start + i + k, :, :128] = jnp.where(keep, zero, own)

    run_pair(0, rows - SPR, SPR, 256, 256)

    edge_out[0, :, :64] = sums[192:, :64]
    edge_out[0, :, 64:] = sums[192:, 192:]
    edge_out[1, :, :64] = sums[128:192, 128:192]
    edge_out[1, :, 64:] = sums[128:192, 64:128]
    edges = both_ways(edge_out, edge_in, edge_send, edge_recv)
    send(edges)

    total = HR + GROUP - SPR
    run_pair(SPR, rows - HR - GROUP, total, 128, 256)

    table_copy.wait()
    for r in range(2, rounds):
        pass_on(r)
    pl.semaphore_wait(vouch.at[rounds - 1], 1)
    for side in range(2):
        @pl.when(receives[side])
        def _():
            edges[side].wait_recv()

        @pl.when(~receives[side])
        def _():
            edge_in[side] = jnp.zeros((nodes, 128), F32)

    early, late = edge_in[0], edge_in[1]
    front0 = jnp.concatenate([sums[64:128, 128:192], sums[64:128, 64:128]], axis=1) + early
    front1 = jnp.concatenate([sums[:64, 64:128], sums[:64, :64] + late[:, :64]], axis=1)
    tails = jnp.concatenate([sums[64:128, :64], sums[:64, 192:] + late[:, 64:]], axis=1)
    lines = nodes // TEAM
    for s in range(TEAM):
        part = slice(s * lines, (s + 1) * lines)
        piece_out[s, : 2 * lines] = jnp.concatenate([front0[part], front1[part]], axis=0).astype(BF16)
        piece_out[s, 2 * lines :] = tails[part].astype(BF16)

    def piece_copy(d):
        there = lax.rem(me + d, count)
        return pltpu.make_async_remote_copy(
            src_ref=piece_out.at[lax.rem(there, TEAM)],
            dst_ref=spread.at[me],
            send_sem=piece_send,
            recv_sem=piece_recv,
            device_id=place_of(there),
            device_id_type=MESH,
        )

    @pl.loop(1, count)
    def _(d):
        piece_copy(d).start()

    spread[me] = piece_out[seat]

    others = spread.at[pl.ds(0, count - 1)]
    all_pieces = pltpu.make_async_remote_copy(
        src_ref=others, dst_ref=others, send_sem=piece_send, recv_sem=piece_recv,
        device_id=after, device_id_type=MESH,
    )
    all_pieces.wait_recv()

    low = lax.broadcasted_iota(jnp.int32, (lines, 128), 1) < 64

    def fill(there, box):
        fronts, ends_of = [], []
        for s in range(OWNMAX):
            entry = table[0, there * OWNMAX + s]
            agg = jnp.maximum(entry - 1, 0)
            which = lax.rem(agg, LW)
            piece = spread[agg // LW].astype(F32)
            front = jnp.where(which == 1, piece[lines : 2 * lines], piece[:lines])
            fronts.append(jnp.where(entry > 0, front, 0.0))
            tail = piece[2 * lines :]
            swapped = jnp.concatenate([tail[:, 64:], tail[:, :64]], axis=1)
            tail = jnp.where(which == s % 2, tail, swapped)
            ends_of.append(jnp.where(entry > 0, tail, 0.0))
        for k in range(OWNMAX // 2):
            box[k] = jnp.concatenate(fronts[2 * k : 2 * k + 2], axis=0).astype(BF16)
        tails = [jnp.where(low, ends_of[2 * k], ends_of[2 * k + 1]) for k in range(OWNMAX // 2)]
        for k in range(OWNMAX // 4):
            box[OWNMAX // 2 + k] = jnp.concatenate(tails[2 * k : 2 * k + 2], axis=0).astype(BF16)

    def mail_copy(d):
        return pltpu.make_async_remote_copy(
            src_ref=mail_out.at[d],
            dst_ref=mail_in.at[seat],
            send_sem=mail_send,
            recv_sem=mail_recv,
            device_id=place_of(mate(d)),
            device_id_type=MESH,
        )

    @pl.loop(1, TEAM, unroll=7)
    def _(d):
        fill(lax.rem(seat + d, TEAM), mail_out.at[d])
        mail_copy(d).start()

    fill(seat, mail_in.at[seat])

    boxes = mail_in.at[pl.ds(0, TEAM - 1)]
    all_mail = pltpu.make_async_remote_copy(
        src_ref=boxes, dst_ref=boxes, send_sem=mail_send, recv_sem=mail_recv,
        device_id=after, device_id_type=MESH,
    )
    all_mail.wait_recv()

    for m in range(TEAM // 2):
        span = pl.ds(2 * lines * m, 2 * lines)
        for k in range(OWNMAX // 2):
            one, two = (mail_in[2 * m + q, k].astype(F32) for q in range(2))
            for h in range(2):
                part = slice(h * lines, (h + 1) * lines)
                out[2 * k + h, span, :128] = jnp.concatenate([one[part], two[part]], axis=0).astype(BF16)
        for k in range(OWNMAX // 4):
            one, two = (mail_in[2 * m + q, OWNMAX // 2 + k].astype(F32) for q in range(2))
            for h in range(2):
                part = slice(h * lines, (h + 1) * lines)
                both = jnp.concatenate([one[part], two[part]], axis=0).astype(BF16)
                out[4 * k + 2 * h, span, 128:] = both[:, :64]
                out[4 * k + 2 * h + 1, span, 128:] = both[:, 64:]

    for side in range(2):
        @pl.when(sends[side])
        def _():
            rims[side].wait_send()
            spills[side].wait_send()
            edges[side].wait_send()

    all_pieces.wait_send()

    all_mail.wait_send()


def shards(a_blocks, a_columns, p_blocks, p_pattern, aggregate, owner_map):
    rows, nodes = a_blocks.shape[:2]
    count = lax.axis_size(AXES)
    vmem = pl.BlockSpec(memory_space=pltpu.VMEM)
    hbm = pl.BlockSpec(memory_space=pl.ANY)
    lines = nodes // TEAM
    half = OWNMAX // 2 + OWNMAX // 4
    dma = pltpu.SemaphoreType.DMA
    pool = (rows + 2 * HR, nodes, 4 * nodes)
    total_agg = owner_map.shape[0]
    return pl.pallas_call(
        kernel,
        out_shape=jax.ShapeDtypeStruct((OWNMAX, nodes, 3 * nodes), BF16),
        in_specs=[hbm] * 6,
        out_specs=vmem,
        scratch_shapes=[
            pltpu.SMEM((a_columns.shape[1], rows), jnp.int32),
            pltpu.SMEM((3, rows), jnp.int32),
            pltpu.SMEM((1, rows), jnp.int32),
            pltpu.VMEM((1, total_agg), jnp.int32),
            pltpu.VMEM(a_blocks.shape, BF16),
            pltpu.VMEM(p_blocks.shape, BF16),
            pltpu.VMEM(pool, BF16),
            pltpu.VMEM((2, (HR + GROUP - SPR) * nodes, 4 * nodes), BF16),
            pltpu.VMEM((4 * nodes, 4 * nodes), F32),
            pltpu.VMEM((2, HR // 2, nodes, 2 * nodes), BF16),
            pltpu.VMEM((2, SPR // 2, nodes, 2 * nodes), BF16),
            pltpu.VMEM((2, HR // 2, nodes, 2 * nodes), BF16),
            pltpu.VMEM((2, SPR // 2, nodes, 2 * nodes), BF16),
            pltpu.VMEM((2, nodes, 2 * nodes), F32),
            pltpu.VMEM((2, nodes, 2 * nodes), F32),
            pltpu.VMEM((TEAM, 3 * lines, 128), BF16),
            pltpu.VMEM((count, 3 * lines, 128), BF16),
            pltpu.VMEM((TEAM, half, 2 * lines, 128), BF16),
            pltpu.VMEM((TEAM, half, 2 * lines, 128), BF16),
            pltpu.VMEM((8, 128), jnp.int32),
            pltpu.SMEM((8, 128), jnp.int32),
            dma((rows // 4 // GROUP + 2,)),
            dma((4,)),
            dma((5,)),
            dma((2,)),
            dma((2,)),
            dma((2,)),
            dma((2,)),
            dma((2,)),
            dma((2,)),
            dma,
            dma,
            dma,
            dma,
            pltpu.SemaphoreType.REGULAR((count.bit_length() - TEAM.bit_length(),)),
        ],
        compiler_params=pltpu.CompilerParams(
            collective_id=0, has_side_effects=True, vmem_limit_bytes=56 << 20
        ),
    )(a_blocks, a_columns.T, p_blocks, p_pattern.T, aggregate[None], owner_map[None])


def solution(mesh):
    placed = (
        P(AXES, None, None),
        P(AXES, None),
        P(AXES, None, None),
        P(AXES, None),
        P(AXES),
        P(),
    )
    return jax.shard_map(
        shards,
        mesh=mesh,
        in_specs=placed,
        out_specs=P(AXES, None, None),
        check_vma=False,
    )
```
